32 devices in a mesh: seq: 32 (over z, y, x, core), head: 1.
Axes of the slice: x: 2, y: 2, z: 4, core: 2. Of those that a mesh axis runs over, the one named last changes fastest.
Arguments:
- tree_queries: bfloat16 [4, 64, 128, 128], P(None, 'seq', 'head'), may hold values from -100 to 100
- tree_keys: bfloat16 [4, 64, 8, 128], P(None, 'seq', 'head'), may hold values from -12 to 12
- tree_values: bfloat16 [4, 64, 8, 128], P(None, 'seq', 'head'), may hold values from -6 to 6
- cache_keys: bfloat16 [4, 20480, 8, 128], P(None, 'seq', 'head'), may hold values from -6 to 6
- cache_values: bfloat16 [4, 20480, 8, 128], P(None, 'seq', 'head'), may hold values from -6 to 6
- out_weight: bfloat16 [16384, 16384], P('head', 'seq'), may hold values from -0.8984375 to 0.8984375
- context_lengths: int32 [4], replicated, may hold values from 2560 to 20472, as said below
- parents: int32 [4, 64], replicated, may hold values from -1 to 62, as said below
- accepted_nodes: int32 [4, 8], replicated, may hold values from 0 to 63, as said below
- accepted_count: int32 [4], replicated, may hold values from 1 to 8
Outputs:
- projected: bfloat16 [256, 16384], P('head', 'seq')
- keys_out: bfloat16 [4, 20480, 8, 128], P(None, 'seq', 'head')
- values_out: bfloat16 [4, 20480, 8, 128], P(None, 'seq', 'head')
The draws below stay inside these ranges and needn't reach their ends.
Inputs may be any that keep to these rules, and one draw needn't show every extreme that they name: Request r's cache holds positions 0 to context_lengths[r] - 1; some request has the largest value in every draw. parents[r, 0] = -1 marks the root; for i >= 1, 0 <= parents[r, i] < i. `accepted_nodes`: each row lists distinct tree nodes in increasing order, the first being the root 0; entries j >= accepted_count[r] are not used.
All inputs are finite; a program needn't handle non-finite values.
Results may differ from the reference program's by a relative error of at most 0.0051.
Values may be sent and summed in bfloat16 or wider, within the bound.
A program may use at most 192 MiB of HBM per device.

```python
import math
import jax
import jax.numpy as jnp
from jax import lax

D = 16384
HQ = 128
KVH = 8
HD = 128
REQ = 4
NODES = 64
ACC = 8
CTX_DEV = 640
CAP = 20480
N_SEQ = 32


def draw_cache_keys(key, part):
    drawn = jnp.clip(jax.random.normal(jax.random.fold_in(key, 21), (REQ, CAP, KVH, HD), jnp.float32), -6.0, 6.0)
    return drawn.astype(jnp.bfloat16)


def draw_tree_queries(key, part):
    drawn = jnp.clip(2.0 * jax.random.normal(jax.random.fold_in(key, 31), (REQ, NODES, HQ, HD), jnp.float32), -12.0, 12.0)
    return drawn.astype(jnp.bfloat16)


def draw_context_lengths(key, part):
    shortest = CAP // 8
    longest = CAP - ACC
    drawn = jax.random.randint(jax.random.fold_in(key, 41), (REQ,), shortest, longest + 1)
    chosen = jax.random.randint(jax.random.fold_in(key, 42), (), 0, REQ)
    return jnp.where(jnp.arange(REQ) == chosen, longest, drawn).astype(jnp.int32)


def draw_parents(key, part):
    bounds = jnp.maximum(jnp.arange(NODES, dtype=jnp.int32), 1)
    drawn = jax.random.randint(jax.random.fold_in(key, 51), (REQ, NODES), 0, bounds[None, :])
    chosen = jax.random.randint(jax.random.fold_in(key, 52), (), 0, REQ)
    last_column = jnp.where(jnp.arange(REQ) == chosen, NODES - 2, drawn[:, NODES - 1])
    drawn = drawn.at[:, NODES - 1].set(last_column)
    return drawn.at[:, 0].set(-1).astype(jnp.int32)


def draw_accepted_nodes(key, part):
    subkeys = jax.random.split(jax.random.fold_in(key, 61), REQ)
    picks = jax.vmap(lambda single: jax.random.permutation(single, NODES - 1)[:ACC - 1] + 1)(subkeys)
    joined = jnp.sort(jnp.concatenate([jnp.zeros((REQ, 1), jnp.int32), picks.astype(jnp.int32)], axis=1), axis=1)
    chosen = jax.random.randint(jax.random.fold_in(key, 62), (), 0, REQ)
    return joined.at[chosen, ACC - 1].set(NODES - 1).astype(jnp.int32)


def draw_accepted_count(key, part):
    drawn = jax.random.randint(jax.random.fold_in(key, 71), (REQ,), 1, ACC + 1)
    chosen = jax.random.randint(jax.random.fold_in(key, 72), (), 0, REQ)
    return jnp.where(jnp.arange(REQ) == chosen, ACC, drawn).astype(jnp.int32)


def levels(stream_key, extent, cuts, least, top_value):
    gain, own = 1.0, jax.random.fold_in(stream_key, 6)
    for position, parts in cuts:
        steps = jnp.exp(jax.random.uniform(jax.random.fold_in(own, position), (parts,), jnp.float32, least / len(cuts), top_value / len(cuts)))
        gain = gain * jnp.repeat(steps, extent[position] // parts).reshape([-1 if axis == position else 1 for axis in range(len(extent))])
    return gain


def bell_draw(stream_key, dims, scale, reach, shards=(), held_as=jnp.bfloat16):
    values = jax.random.normal(stream_key, dims, jnp.float32) * scale
    if len(shards) > 0:
        values = levels(stream_key, dims, shards, -0.22, 0.18) * values
    return jnp.clip(values, min=-reach, max=reach).astype(held_as)


def setup_inputs(seed: int = 0) -> dict:
    seeds = jax.random.split(jax.random.key(seed), 11)
    return {
        "tree_queries": draw_tree_queries(jax.random.fold_in(seeds[10], 71), 0),
        "tree_keys": bell_draw(seeds[1], (REQ, NODES, KVH, HD), 2.0, 12.0, ((1, 32),)),
        "tree_values": bell_draw(seeds[2], (REQ, NODES, KVH, HD), 1.0, 6.0, ((1, 32),)),
        "cache_keys": draw_cache_keys(jax.random.fold_in(seeds[10], 71), 0),
        "cache_values": bell_draw(seeds[4], (REQ, CAP, KVH, HD), 1.0, 6.0, ((1, 32),)),
        "out_weight": bell_draw(seeds[5], (HQ * HD, D), 0.15, 0.8984375, ((1, 32),)),
        "context_lengths": draw_context_lengths(jax.random.fold_in(seeds[10], 71), 0),
        "parents": draw_parents(jax.random.fold_in(seeds[10], 71), 0),
        "accepted_nodes": draw_accepted_nodes(jax.random.fold_in(seeds[10], 71), 0),
        "accepted_count": draw_accepted_count(jax.random.fold_in(seeds[10], 71), 0),
    }


NEG = -1e+30

def ancestors(parents):
    count_nodes = parents.shape[1]
    columns = jnp.arange(count_nodes, dtype=jnp.int32)
    linked = (parents[:, :, None] == columns[None, None, :]) | (columns[:, None] == columns[None, :])[None]
    closure = linked.astype(jnp.float32)
    for rounds in range(max(count_nodes - 1, 1).bit_length()):
        closure = jnp.minimum(jnp.matmul(closure, closure, precision=lax.Precision.HIGHEST), 1.0)
    return closure

def reference(tree_queries, tree_keys, tree_values, cache_keys, cache_values, out_weight, context_lengths, parents, accepted_nodes, accepted_count):
    scale_factor = 1.0 / math.sqrt(HD)
    group_size = HQ // KVH
    closure = ancestors(parents)
    outputs = []
    for request in range(REQ):
        grouped = tree_queries[request].astype(jnp.float32).reshape(NODES, KVH, group_size, HD)
        cache_k = cache_keys[request].astype(jnp.float32).reshape(N_SEQ, CTX_DEV, KVH, HD)
        cache_v = cache_values[request].astype(jnp.float32).reshape(N_SEQ, CTX_DEV, KVH, HD)
        tree_k = tree_keys[request].astype(jnp.float32)
        tree_v = tree_values[request].astype(jnp.float32)
        in_cache = (jnp.arange(CAP, dtype=jnp.int32) < context_lengths[request]).reshape(N_SEQ, CTX_DEV)
        tree_allowed = closure[request] > 0.5

        def per_head(operands):
            queries, keys_c, values_c, keys_t, values_t = operands
            scores_c = jnp.einsum('ngd,bpd->ngbp', queries, keys_c) * scale_factor
            mask_c = in_cache[None, None, :, :]
            top_c = lax.optimization_barrier(jnp.max(jnp.where(mask_c, scores_c, NEG), axis=-1))
            weights_c = jnp.where(mask_c, jnp.exp(scores_c - top_c[..., None]), 0.0)
            scores_t = jnp.einsum('ngd,pd->ngp', queries, keys_t) * scale_factor
            mask_t = tree_allowed[:, None, :]
            top_t = lax.optimization_barrier(jnp.max(jnp.where(mask_t, scores_t, NEG), axis=-1))
            weights_t = jnp.where(mask_t, jnp.exp(scores_t - top_t[..., None]), 0.0)
            row_top = jnp.maximum(lax.optimization_barrier(jnp.max(top_c, axis=-1)), top_t)
            factor_c = jnp.exp(top_c - row_top[..., None])
            factor_t = jnp.exp(top_t - row_top)
            row_sum = lax.optimization_barrier(jnp.sum(lax.optimization_barrier(jnp.sum(weights_c, axis=-1)) * factor_c, axis=-1)) + lax.optimization_barrier(jnp.sum(weights_t, axis=-1)) * factor_t
            rounded_c = lax.optimization_barrier(weights_c.astype(jnp.bfloat16)).astype(jnp.float32)
            rounded_t = lax.optimization_barrier(weights_t.astype(jnp.bfloat16)).astype(jnp.float32)
            block_num = jnp.einsum('ngbp,bpd->ngbd', rounded_c, values_c)
            numerator = lax.optimization_barrier(jnp.sum(block_num * factor_c[..., None], axis=2))
            numerator = numerator + jnp.einsum('ngp,pd->ngd', rounded_t, values_t) * factor_t[..., None]
            return (numerator / row_sum[:, :, None]).astype(jnp.bfloat16)
        per_head_out = lax.map(per_head, (jnp.moveaxis(grouped, 1, 0), jnp.moveaxis(cache_k, 2, 0), jnp.moveaxis(cache_v, 2, 0), jnp.moveaxis(tree_k, 1, 0), jnp.moveaxis(tree_v, 1, 0)))
        outputs.append(jnp.moveaxis(per_head_out, 0, 1).reshape(NODES, HQ * HD))
    attention = jnp.concatenate(outputs, axis=0)
    projected = jnp.dot(attention, out_weight, preferred_element_type=jnp.float32).astype(jnp.bfloat16)
    rows_index = jnp.arange(REQ, dtype=jnp.int32)[:, None]
    steps_index = jnp.arange(ACC, dtype=jnp.int32)[None, :]
    targets = jnp.where(steps_index < accepted_count[:, None], context_lengths[:, None] + steps_index, CAP).astype(jnp.int32)
    keys_out = cache_keys.at[rows_index, targets].set(tree_keys[rows_index, accepted_nodes], mode='drop')
    values_out = cache_values.at[rows_index, targets].set(tree_values[rows_index, accepted_nodes], mode='drop')
    return (projected, keys_out, values_out)
```

```python
import functools
import math

import jax
import jax.numpy as jnp
from jax import lax
from jax.experimental import pallas as pl
from jax.experimental.pallas import tpu as pltpu
from jax.sharding import PartitionSpec as P

NEG = -1e30


def ancestors(parents):
    count_nodes = parents.shape[1]
    columns = jnp.arange(count_nodes, dtype=jnp.int32)
    linked = (parents[:, :, None] == columns[None, None, :]) | (
        columns[:, None] == columns[None, :]
    )[None]
    closure = linked.astype(jnp.float32)
    for rounds in range(max(count_nodes - 1, 1).bit_length()):
        closure = jnp.minimum(jnp.matmul(closure, closure, precision=lax.Precision.HIGHEST), 1.0)
    return closure


def partial_attention(queries, keys, values, allowed, scale_factor):
    scores = (
        jnp.einsum("rnhge,rphe->rnhgp", queries, keys, preferred_element_type=jnp.float32)
        * scale_factor
    )
    row_top = jnp.max(jnp.where(allowed, scores, NEG), axis=-1)
    weights = jnp.where(allowed, jnp.exp(scores - row_top[..., None]), 0.0)
    row_sum = jnp.sum(weights, axis=-1)
    numerator = jnp.einsum(
        "rnhgp,rphe->rnhge",
        weights.astype(jnp.bfloat16),
        values,
        preferred_element_type=jnp.float32,
    )
    return (row_top, row_sum, numerator)


def merge_parts(first, second):
    top_first, sum_first, acc_first = first
    top_second, sum_second, acc_second = second
    row_top = jnp.maximum(top_first, top_second)
    scale_first = jnp.exp(top_first - row_top)
    scale_second = jnp.exp(top_second - row_top)
    row_sum = sum_first * scale_first + sum_second * scale_second
    numerator = acc_first * scale_first[..., None] + acc_second * scale_second[..., None]
    return (row_top, row_sum, numerator)


def append_rows(cache_block, tree_all, choose, slot_map, written):
    picked = jnp.einsum(
        "rjn,rnhe->rjhe", choose, tree_all, preferred_element_type=jnp.float32
    ).astype(jnp.bfloat16)
    placed = jnp.einsum(
        "rjp,rjhe->rphe", slot_map, picked, preferred_element_type=jnp.float32
    ).astype(jnp.bfloat16)
    return jnp.where(written[:, :, None, None], placed, cache_block)


def on_device_plain(
    tree_queries,
    tree_keys,
    tree_values,
    cache_keys,
    cache_values,
    out_weight,
    context_lengths,
    parents,
    accepted_nodes,
    accepted_count,
):
    requests, ctx_local, kv_local, head_dim = cache_keys.shape
    node_local, q_local = (tree_queries.shape[1], tree_queries.shape[2])
    group_size = q_local // kv_local
    path_len = accepted_nodes.shape[1]
    scale_factor = 1.0 / math.sqrt(head_dim)
    seq_index = lax.axis_index("seq")
    seq_count = lax.axis_size("seq")
    nodes_all = node_local * seq_count
    offset = seq_index * ctx_local
    grouped = tree_queries.reshape(requests, node_local, kv_local, group_size, head_dim)
    tree_all_k, tree_all_v = (
        lax.all_gather(tree_keys, "seq", axis=1, tiled=True),
        lax.all_gather(tree_values, "seq", axis=1, tiled=True),
    )
    closure = ancestors(parents)
    home_rows = lax.dynamic_slice_in_dim(closure, seq_index * node_local, node_local, 1)
    tree_state = partial_attention(
        grouped, tree_all_k, tree_all_v, home_rows[:, :, None, None, :] > 0.5, scale_factor
    )
    positions = offset + jnp.arange(ctx_local, dtype=jnp.int32)
    usable = (positions[None, :] < context_lengths[:, None])[:, None, None, None, :]
    everyone = lax.all_gather(grouped, "seq", axis=1, tiled=True)
    row_top, row_sum, numerator = partial_attention(
        everyone, cache_keys, cache_values, usable, scale_factor
    )
    highest = lax.pmax(row_top, "seq")
    factor = jnp.exp(row_top - highest)
    summed_acc, summed_sum = (
        lax.psum_scatter(numerator * factor[..., None], "seq", scatter_dimension=1, tiled=True),
        lax.psum_scatter(row_sum * factor, "seq", scatter_dimension=1, tiled=True),
    )
    home_top = lax.dynamic_slice_in_dim(highest, seq_index * node_local, node_local, 1)
    cache_state = (home_top, summed_sum, summed_acc)
    final_top, final_sum, final_acc = merge_parts(cache_state, tree_state)
    attention = (
        (final_acc / final_sum[..., None])
        .astype(jnp.bfloat16)
        .reshape(requests, node_local, q_local * head_dim)
    )
    partial_terms = jnp.einsum(
        "rnx,xd->rnd",
        lax.all_gather(attention, "seq", axis=1, tiled=True),
        out_weight,
        preferred_element_type=jnp.float32,
    )
    partial_terms = partial_terms.reshape(requests * nodes_all, out_weight.shape[1])
    projected = lax.psum_scatter(partial_terms, "head", scatter_dimension=0, tiled=True).astype(
        jnp.bfloat16
    )
    choose = (
        accepted_nodes[:, :, None] == jnp.arange(nodes_all, dtype=jnp.int32)[None, None, :]
    ).astype(jnp.bfloat16)
    steps_index = jnp.arange(path_len, dtype=jnp.int32)
    targets = context_lengths[:, None] + steps_index[None, :] - offset
    alive = steps_index[None, :] < accepted_count[:, None]
    slot_flags = (
        targets[:, :, None] == jnp.arange(ctx_local, dtype=jnp.int32)[None, None, :]
    ) & alive[:, :, None]
    slot_map = slot_flags.astype(jnp.bfloat16)
    written = jnp.sum(slot_flags.astype(jnp.float32), axis=1) > 0.5
    keys_out = append_rows(cache_keys, tree_all_k, choose, slot_map, written)
    values_out = append_rows(cache_values, tree_all_v, choose, slot_map, written)
    return (projected, keys_out, values_out)


MESH = pl.DeviceIdType.MESH
LOG2E = math.log2(math.e)


def bit_of(me, bit):
    return (me // (1 << bit)) % 2


def partner_of(me, bit):
    return me + (1 - 2 * bit_of(me, bit)) * (1 << bit)


def greet(me, levels):
    barrier = pltpu.get_barrier_semaphore()
    for bit in range(levels):
        pl.semaphore_signal(
            barrier, inc=1, device_id={"seq": partner_of(me, bit)}, device_id_type=MESH
        )
    pl.semaphore_wait(barrier, levels)


def gather_orders(levels):
    high = list(range(levels - 1, 2, -1))
    return (high + [1, 2, 0], high + [2, 1, 0])


def gather_kernel(levels, chunks, mine, out, own_sem, send_sem, recv_sem):
    me = lax.axis_index("seq")
    orders = gather_orders(levels)
    own = [bit_of(me, bit) for bit in range(levels)]
    greet(me, levels)

    def copy(c, p, half):
        done = orders[half][:p]
        where = tuple(
            slice(None) if bit in done else own[bit] for bit in range(levels - 1, -1, -1)
        )
        place = out.at[(c,) + where + (half,)]
        return pltpu.make_async_remote_copy(
            src_ref=mine.at[c, half] if p == 0 else place,
            dst_ref=place,
            send_sem=send_sem.at[c, p, half],
            recv_sem=recv_sem.at[c, p, half],
            device_id={"seq": partner_of(me, orders[half][p])},
            device_id_type=MESH,
        )

    mine_bits = tuple(own[bit] for bit in range(levels - 1, -1, -1))
    locals_ = [
        pltpu.make_async_copy(mine.at[c], out.at[(c,) + mine_bits], own_sem.at[c])
        for c in range(chunks)
    ]
    copies = {}
    for c in range(chunks):
        for half in range(2):
            copies[c, 0, half] = copy(c, 0, half)
            copies[c, 0, half].start()
    for c in range(chunks):
        locals_[c].start()
    for step in range(chunks + levels):
        for p in range(levels, 0, -1):
            c = step - p
            if not 0 <= c < chunks:
                continue
            if p == 1:
                locals_[c].wait()
            for half in range(2):
                copies[c, p - 1, half].wait_recv()
                if p < levels:
                    copies[c, p, half] = copy(c, p, half)
                    copies[c, p, half].start()
    for pending in copies.values():
        pending.wait_send()


def gather(block, count, collective_id):
    chunks = block.shape[0]
    levels = count.bit_length() - 1
    out = pl.pallas_call(
        functools.partial(gather_kernel, levels, chunks),
        out_shape=jax.ShapeDtypeStruct(
            (chunks,) + (2,) * levels + block.shape[1:], block.dtype
        ),
        in_specs=[pl.BlockSpec(memory_space=pl.ANY)],
        out_specs=pl.BlockSpec(memory_space=pl.ANY),
        scratch_shapes=[
            pltpu.SemaphoreType.DMA((chunks,)),
            pltpu.SemaphoreType.DMA((chunks, levels, 2)),
            pltpu.SemaphoreType.DMA((chunks, levels, 2)),
        ],
        compiler_params=pltpu.CompilerParams(
            collective_id=collective_id, has_side_effects=True
        ),
    )(block)
    return out.reshape((chunks, count) + block.shape[1:])


def scatter_kernel(levels, chunks, acc, logs, out, work, work_s, load_sem, send_sem, recv_sem, *recv):
    me = lax.axis_index("seq")
    orders = tuple(order[::-1] for order in gather_orders(levels))
    own = [bit_of(me, bit) for bit in range(levels)]
    held, held_s = recv[:levels], recv[levels:]
    rows = out.shape[2]
    loads = []
    for c in range(chunks):
        loads.append(pltpu.make_async_copy(acc.at[c], work.at[c], load_sem.at[0, c]))
        loads.append(pltpu.make_async_copy(logs.at[c], work_s.at[c], load_sem.at[1, c]))
    for load in loads:
        load.start()
    greet(me, levels)

    def send(c, p, half):
        bit_now = orders[half][p]
        done = orders[half][:p]
        where = []
        for bit in range(levels - 1, -1, -1):
            if bit in done:
                where.append(own[bit])
            elif bit == bit_now:
                where.append(1 - own[bit])
            else:
                where.append(slice(None))
        place = (c,) + tuple(where) + (half,)
        made = []
        for kind, (source, target) in enumerate(((work, held[p]), (work_s, held_s[p]))):
            made.append(
                pltpu.make_async_remote_copy(
                    src_ref=source.at[place],
                    dst_ref=target.at[c, half],
                    send_sem=send_sem.at[kind, c, p, half],
                    recv_sem=recv_sem.at[kind, c, p, half],
                    device_id={"seq": partner_of(me, bit_now)},
                    device_id_type=MESH,
                )
            )
        for one in made:
            one.start()
        return made

    row_id = lax.broadcasted_iota(jnp.int32, (rows, rows), 0)
    column_id = lax.broadcasted_iota(jnp.int32, (rows, rows), 1)
    diagonal = row_id == column_id

    def merge(c, p, half):
        done = orders[half][: p + 1]
        free = [bit for bit in range(levels - 1, -1, -1) if bit not in done]
        last = p == levels - 1

        def body(k, carry):
            place, there, rank = [], [], len(free)
            for bit in range(levels - 1, -1, -1):
                if bit in done:
                    place.append(own[bit])
                else:
                    rank -= 1
                    digit = (k // (1 << rank)) % 2
                    place.append(digit)
                    there.append(digit)
            at_work = (c,) + tuple(place) + (half,)
            at_held = (c, half) + tuple(there)
            log_a, log_b = work_s[at_work], held_s[p][at_held]
            top = jnp.maximum(log_a, log_b)
            part_a, part_b = jnp.exp2(log_a - top), jnp.exp2(log_b - top)
            total = part_a + part_b
            share = jnp.sum(
                jnp.where(diagonal, part_a / total, 0.0), axis=1, keepdims=True
            )
            merged = (
                work[at_work].astype(jnp.float32) * share
                + held[p][at_held].astype(jnp.float32) * (1.0 - share)
            ).astype(jnp.bfloat16)
            if last:
                out[c, half] = merged
            else:
                work[at_work] = merged
                work_s[at_work] = top + jnp.log2(total)
            return carry

        if free:
            lax.fori_loop(0, 1 << len(free), body, 0)
        else:
            body(0, 0)

    copies = {}
    for c in range(chunks):
        loads[2 * c].wait()
        loads[2 * c + 1].wait()
        for half in range(2):
            copies[c, 0, half] = send(c, 0, half)
    for step in range(chunks + levels):
        for p in range(levels, 0, -1):
            c = step - p
            if not 0 <= c < chunks:
                continue
            for half in range(2):
                for one in copies[c, p - 1, half]:
                    one.wait_recv()
                merge(c, p - 1, half)
                if p < levels:
                    copies[c, p, half] = send(c, p, half)
    for pair in copies.values():
        for one in pair:
            one.wait_send()


def scatter_merge(acc, logs, count, collective_id):
    chunks, _, _, rows, width = acc.shape
    levels = count.bit_length() - 1
    bits = (2,) * levels
    held = [pltpu.VMEM((chunks, 2) + bits[: levels - 1 - p] + (rows, width), jnp.bfloat16) for p in range(levels)]
    held_s = [pltpu.VMEM((chunks, 2) + bits[: levels - 1 - p] + (1, rows), jnp.float32) for p in range(levels)]
    return pl.pallas_call(
        functools.partial(scatter_kernel, levels, chunks),
        out_shape=jax.ShapeDtypeStruct((chunks, 2, rows, width), jnp.bfloat16),
        in_specs=[pl.BlockSpec(memory_space=pl.ANY)] * 2,
        out_specs=pl.BlockSpec(memory_space=pltpu.VMEM),
        scratch_shapes=[
            pltpu.VMEM((chunks,) + bits + (2, rows, width), jnp.bfloat16),
            pltpu.VMEM((chunks,) + bits + (2, 1, rows), jnp.float32),
            pltpu.SemaphoreType.DMA((2, chunks)),
            pltpu.SemaphoreType.DMA((2, chunks, levels, 2)),
            pltpu.SemaphoreType.DMA((2, chunks, levels, 2)),
        ]
        + held
        + held_s,
        compiler_params=pltpu.CompilerParams(
            collective_id=collective_id, has_side_effects=True, vmem_limit_bytes=48 * 2**20
        ),
    )(acc.reshape((chunks,) + bits + (2, rows, width)), logs.reshape((chunks,) + bits + (2, 1, rows)))


def attend_kernel(
    scale, where, lengths, accepted, count,
    q, k, v, tree_k, tree_v, own_k, own_v, own_bias,
    acc, logs, k_out, v_out, k_wide, v_wide,
):
    r, h = pl.program_id(0), pl.program_id(1)
    ctx, kv, width = k.shape[1:]
    nodes, group = q.shape[1:3]
    me, offset = where[0], where[1]

    @pl.when(h == 0)
    def _():
        for cache, wide, fresh, target in ((k, k_wide, tree_k, k_out), (v, v_wide, tree_v, v_out)):
            wide[...] = cache[0].astype(jnp.float32).reshape(ctx * kv, width)
            target[...] = cache[...]
            for j in range(accepted.shape[1]):
                slot = lengths[r] + j - offset

                @pl.when((j < count[r]) & (slot >= 0) & (slot < ctx))
                def _():
                    target[0, slot] = fresh[0, accepted[r, j]]

    keys = k_wide[pl.ds(h, ctx, stride=kv), :].astype(jnp.bfloat16)
    values = v_wide[pl.ds(h, ctx, stride=kv), :].astype(jnp.bfloat16)
    position = offset + lax.broadcasted_iota(jnp.int32, (1, ctx), 1)
    bias = jnp.where(position < lengths[r], 0.0, NEG)
    queries = q[0].reshape(nodes * group, width)
    tile = 2 * width
    diagonal = lax.broadcasted_iota(jnp.int32, (width, width), 0) == lax.broadcasted_iota(
        jnp.int32, (width, width), 1
    )

    def block(rows, key, value, bias):
        scores = lax.dot_general(
            rows, key, (((1,), (1,)), ((), ())), preferred_element_type=jnp.float32
        )
        scores = scores * (scale * LOG2E) + bias
        top = jnp.max(scores, axis=1, keepdims=True)
        weights = jnp.exp2(scores - top)
        total = jnp.sum(weights, axis=1, keepdims=True)
        number = jnp.dot(weights.astype(jnp.bfloat16), value, preferred_element_type=jnp.float32)
        return top, total, number

    def store(start, top, total, number):
        acc[0, start : start + tile] = (number / total).astype(jnp.bfloat16)
        lines = top + jnp.log2(total)
        for part in range(tile // width):
            line = jnp.sum(
                jnp.where(diagonal, lines[part * width : (part + 1) * width], 0.0),
                axis=0,
                keepdims=True,
            )
            at = start // width + part
            logs[0, at : at + 1, :] = line

    has_tree = (r * kv + h) == me
    for start in range(0, nodes * group, tile):
        rows = queries[start : start + tile]
        top, total, number = block(rows, keys, values, bias)
        store(start, top, total, number)

    @pl.when(has_tree)
    def _():
        for start in range(0, nodes * group, tile):
            rows = queries[start : start + tile]
            top, total, number = block(rows, keys, values, bias)
            t_top, t_total, t_number = block(
                rows, own_k[...], own_v[...], own_bias[start : start + tile]
            )
            high = jnp.maximum(top, t_top)
            fa, fb = jnp.exp2(top - high), jnp.exp2(t_top - high)
            store(start, high, total * fa + t_total * fb, number * fa + t_number * fb)


def attend(scale, where, lengths, accepted, count, q_all, k, v, tree_k, tree_v, own_k, own_v, own_bias):
    requests, ctx, kv, width = k.shape
    nodes = q_all.shape[1]
    group = own_bias.shape[0] // nodes
    rows = nodes * group
    whole = pl.BlockSpec(memory_space=pltpu.VMEM)
    by_request = lambda r, h, *_: (r, 0, 0, 0)
    cache_spec = pl.BlockSpec((1, ctx, kv, width), by_request)
    tree_spec = pl.BlockSpec((1, nodes, kv, width), by_request)
    work = requests * kv * rows * ctx
    return pl.pallas_call(
        functools.partial(attend_kernel, scale),
        grid_spec=pltpu.PrefetchScalarGridSpec(
            num_scalar_prefetch=4,
            grid=(requests, kv),
            in_specs=[
                pl.BlockSpec((1, nodes, group, width), lambda r, h, *_: (r, 0, h, 0)),
                cache_spec, cache_spec, tree_spec, tree_spec, whole, whole, whole,
            ],
            out_specs=[
                pl.BlockSpec((1, rows, width), lambda r, h, *_: (r, h, 0)),
                pl.BlockSpec((1, rows // width, width), lambda r, h, *_: (r, h, 0)),
                cache_spec, cache_spec,
            ],
            scratch_shapes=[pltpu.VMEM((ctx * kv, width), jnp.float32)] * 2,
        ),
        out_shape=[
            jax.ShapeDtypeStruct((requests, kv * rows, width), jnp.bfloat16),
            jax.ShapeDtypeStruct((requests, kv * rows // width, width), jnp.float32),
            jax.ShapeDtypeStruct(k.shape, k.dtype),
            jax.ShapeDtypeStruct(v.shape, v.dtype),
        ],
        compiler_params=pltpu.CompilerParams(vmem_limit_bytes=48 * 2**20),
        cost_estimate=pl.CostEstimate(
            flops=4 * work * width, bytes_accessed=4 * k.size * 2, transcendentals=work
        ),
    )(where, lengths, accepted, count, q_all, k, v, tree_k, tree_v, own_k, own_v, own_bias)


def project_kernel(a, w, out, total):
    step = pl.program_id(0)

    @pl.when(step == 0)
    def _():
        total[...] = jnp.zeros_like(total)

    requests, _, parts, group, some, width = a.shape
    rows = requests * parts * some
    term = None
    for g in range(0, group, 2):
        left = jnp.concatenate(
            [a[:, 0, :, g + i].reshape(rows, width) for i in range(2)], axis=1
        )
        now = jnp.dot(
            left, w[g * width : (g + 2) * width, :], preferred_element_type=jnp.float32
        )
        term = now if term is None else term + now
    total[...] += term

    @pl.when(step == pl.num_programs(0) - 1)
    def _():
        out[...] = total[...].astype(out.dtype)


def project(attention, weight):
    requests, kv, parts, group, some, width = attention.shape
    rows = requests * parts * some
    columns = weight.shape[1]
    return pl.pallas_call(
        project_kernel,
        grid=(kv,),
        in_specs=[
            pl.BlockSpec((requests, 1, parts, group, some, width), lambda h: (0, h, 0, 0, 0, 0)),
            pl.BlockSpec((group * width, columns), lambda h: (h, 0)),
        ],
        out_specs=pl.BlockSpec((rows, columns), lambda h: (0, 0)),
        out_shape=jax.ShapeDtypeStruct((rows, columns), jnp.bfloat16),
        scratch_shapes=[pltpu.VMEM((rows, columns), jnp.float32)],
        compiler_params=pltpu.CompilerParams(vmem_limit_bytes=40 * 2**20),
    )(attention, weight)


def on_device(
    tree_queries,
    tree_keys,
    tree_values,
    cache_keys,
    cache_values,
    out_weight,
    context_lengths,
    parents,
    accepted_nodes,
    accepted_count,
):
    requests, ctx, kv, width = cache_keys.shape
    node_local, heads = tree_queries.shape[1:3]
    group = heads // kv
    count = lax.axis_size("seq")
    nodes = node_local * count
    part = kv * nodes // count
    me = lax.axis_index("seq")
    sent = jnp.concatenate([tree_queries, tree_keys, tree_values], axis=2)
    closure = ancestors(parents)
    everyone = gather(sent, count, 1).reshape(requests, nodes, heads + 2 * kv, width)
    tree_k = everyone[:, :, heads : heads + kv]
    tree_v = everyone[:, :, heads + kv :]
    pair = lax.rem(me, requests * kv)
    own_request, own_head = pair // kv, lax.rem(pair, kv)
    own_k = lax.dynamic_slice(tree_k, (own_request, 0, own_head, 0), (1, nodes, 1, width))
    own_v = lax.dynamic_slice(tree_v, (own_request, 0, own_head, 0), (1, nodes, 1, width))
    own_reach = lax.dynamic_index_in_dim(closure, own_request, 0, keepdims=False)
    own_bias = jnp.repeat(jnp.where(own_reach > 0.5, 0.0, NEG), group, axis=0)
    acc, logs, keys_out, values_out = attend(
        1.0 / math.sqrt(width),
        jnp.stack([me, me * ctx]).astype(jnp.int32),
        context_lengths, accepted_nodes, accepted_count,
        everyone, cache_keys, cache_values, tree_k, tree_v,
        own_k.reshape(nodes, width), own_v.reshape(nodes, width), own_bias,
    )
    half_rows = part * group // 2
    home = scatter_merge(
        acc.reshape(requests, count, 2, half_rows, width),
        logs.reshape(requests, count, 2, 1, half_rows),
        count,
        2,
    )
    home = home.reshape(requests, part, group, width).swapaxes(1, 2)
    attention = gather(home.reshape(requests, 2, half_rows, width), count, 3)
    attention = attention.reshape(requests, kv, count // kv, group, part, width)
    return (project(attention, out_weight), keys_out, values_out)


def fits(mesh, args):
    queries, keys = args[0], args[3]
    count, split = mesh.shape["seq"], mesh.shape["head"]
    requests, nodes, heads, width = queries.shape
    kv = keys.shape[2]
    rows = nodes * heads // count
    return (
        split == 1
        and count >= 8
        and count & (count - 1) == 0
        and count % kv == 0
        and count >= requests * kv
        and nodes * kv // count % 16 == 0
        and nodes == 2 * count
        and rows == 2 * width
    )


def solution(mesh):
    in_specs = (
        P(None, "seq", "head", None),
        P(None, "seq", "head", None),
        P(None, "seq", "head", None),
        P(None, "seq", "head", None),
        P(None, "seq", "head", None),
        P("head", "seq"),
        P(),
        P(),
        P(),
        P(),
    )
    out_specs = (P("head", "seq"), P(None, "seq", "head", None), P(None, "seq", "head", None))

    def run(*args):
        body = on_device if fits(mesh, args) else on_device_plain
        return jax.shard_map(
            body, mesh=mesh, in_specs=in_specs, out_specs=out_specs, check_vma=False
        )(*args)

    return run
```

```python
import functools
import math

import jax
import jax.numpy as jnp
from jax import lax
from jax.experimental import pallas as pl
from jax.experimental.pallas import tpu as pltpu
from jax.sharding import PartitionSpec as P

NEG = -1e30


def ancestors(parents):
    count_nodes = parents.shape[1]
    columns = jnp.arange(count_nodes, dtype=jnp.int32)
    linked = (parents[:, :, None] == columns[None, None, :]) | (
        columns[:, None] == columns[None, :]
    )[None]
    closure = linked.astype(jnp.float32)
    for rounds in range(max(count_nodes - 1, 1).bit_length()):
        closure = jnp.minimum(jnp.matmul(closure, closure, precision=lax.Precision.HIGHEST), 1.0)
    return closure


def partial_attention(queries, keys, values, allowed, scale_factor):
    scores = (
        jnp.einsum("rnhge,rphe->rnhgp", queries, keys, preferred_element_type=jnp.float32)
        * scale_factor
    )
    row_top = jnp.max(jnp.where(allowed, scores, NEG), axis=-1)
    weights = jnp.where(allowed, jnp.exp(scores - row_top[..., None]), 0.0)
    row_sum = jnp.sum(weights, axis=-1)
    numerator = jnp.einsum(
        "rnhgp,rphe->rnhge",
        weights.astype(jnp.bfloat16),
        values,
        preferred_element_type=jnp.float32,
    )
    return (row_top, row_sum, numerator)


def merge_parts(first, second):
    top_first, sum_first, acc_first = first
    top_second, sum_second, acc_second = second
    row_top = jnp.maximum(top_first, top_second)
    scale_first = jnp.exp(top_first - row_top)
    scale_second = jnp.exp(top_second - row_top)
    row_sum = sum_first * scale_first + sum_second * scale_second
    numerator = acc_first * scale_first[..., None] + acc_second * scale_second[..., None]
    return (row_top, row_sum, numerator)


def append_rows(cache_block, tree_all, choose, slot_map, written):
    picked = jnp.einsum(
        "rjn,rnhe->rjhe", choose, tree_all, preferred_element_type=jnp.float32
    ).astype(jnp.bfloat16)
    placed = jnp.einsum(
        "rjp,rjhe->rphe", slot_map, picked, preferred_element_type=jnp.float32
    ).astype(jnp.bfloat16)
    return jnp.where(written[:, :, None, None], placed, cache_block)


def on_device_plain(
    tree_queries,
    tree_keys,
    tree_values,
    cache_keys,
    cache_values,
    out_weight,
    context_lengths,
    parents,
    accepted_nodes,
    accepted_count,
):
    requests, ctx_local, kv_local, head_dim = cache_keys.shape
    node_local, q_local = (tree_queries.shape[1], tree_queries.shape[2])
    group_size = q_local // kv_local
    path_len = accepted_nodes.shape[1]
    scale_factor = 1.0 / math.sqrt(head_dim)
    seq_index = lax.axis_index("seq")
    seq_count = lax.axis_size("seq")
    nodes_all = node_local * seq_count
    offset = seq_index * ctx_local
    grouped = tree_queries.reshape(requests, node_local, kv_local, group_size, head_dim)
    tree_all_k, tree_all_v = (
        lax.all_gather(tree_keys, "seq", axis=1, tiled=True),
        lax.all_gather(tree_values, "seq", axis=1, tiled=True),
    )
    closure = ancestors(parents)
    home_rows = lax.dynamic_slice_in_dim(closure, seq_index * node_local, node_local, 1)
    tree_state = partial_attention(
        grouped, tree_all_k, tree_all_v, home_rows[:, :, None, None, :] > 0.5, scale_factor
    )
    positions = offset + jnp.arange(ctx_local, dtype=jnp.int32)
    usable = (positions[None, :] < context_lengths[:, None])[:, None, None, None, :]
    everyone = lax.all_gather(grouped, "seq", axis=1, tiled=True)
    row_top, row_sum, numerator = partial_attention(
        everyone, cache_keys, cache_values, usable, scale_factor
    )
    highest = lax.pmax(row_top, "seq")
    factor = jnp.exp(row_top - highest)
    summed_acc, summed_sum = (
        lax.psum_scatter(numerator * factor[..., None], "seq", scatter_dimension=1, tiled=True),
        lax.psum_scatter(row_sum * factor, "seq", scatter_dimension=1, tiled=True),
    )
    home_top = lax.dynamic_slice_in_dim(highest, seq_index * node_local, node_local, 1)
    cache_state = (home_top, summed_sum, summed_acc)
    final_top, final_sum, final_acc = merge_parts(cache_state, tree_state)
    attention = (
        (final_acc / final_sum[..., None])
        .astype(jnp.bfloat16)
        .reshape(requests, node_local, q_local * head_dim)
    )
    partial_terms = jnp.einsum(
        "rnx,xd->rnd",
        lax.all_gather(attention, "seq", axis=1, tiled=True),
        out_weight,
        preferred_element_type=jnp.float32,
    )
    partial_terms = partial_terms.reshape(requests * nodes_all, out_weight.shape[1])
    projected = lax.psum_scatter(partial_terms, "head", scatter_dimension=0, tiled=True).astype(
        jnp.bfloat16
    )
    choose = (
        accepted_nodes[:, :, None] == jnp.arange(nodes_all, dtype=jnp.int32)[None, None, :]
    ).astype(jnp.bfloat16)
    steps_index = jnp.arange(path_len, dtype=jnp.int32)
    targets = context_lengths[:, None] + steps_index[None, :] - offset
    alive = steps_index[None, :] < accepted_count[:, None]
    slot_flags = (
        targets[:, :, None] == jnp.arange(ctx_local, dtype=jnp.int32)[None, None, :]
    ) & alive[:, :, None]
    slot_map = slot_flags.astype(jnp.bfloat16)
    written = jnp.sum(slot_flags.astype(jnp.float32), axis=1) > 0.5
    keys_out = append_rows(cache_keys, tree_all_k, choose, slot_map, written)
    values_out = append_rows(cache_values, tree_all_v, choose, slot_map, written)
    return (projected, keys_out, values_out)


MESH = pl.DeviceIdType.MESH
LOG2E = math.log2(math.e)


def bit_of(me, bit):
    return (me // (1 << bit)) % 2


def partner_of(me, bit):
    return me + (1 - 2 * bit_of(me, bit)) * (1 << bit)


def greet(me, levels):
    barrier = pltpu.get_barrier_semaphore()
    for bit in range(levels):
        pl.semaphore_signal(
            barrier, inc=1, device_id={"seq": partner_of(me, bit)}, device_id_type=MESH
        )
    pl.semaphore_wait(barrier, levels)


def gather_orders(levels):
    high = list(range(levels - 1, 2, -1))
    return (high + [1, 2, 0], high + [2, 1, 0])


def digits_of(value, levels):
    return tuple((value // (1 << bit)) % 2 for bit in range(levels - 1, -1, -1))


def gather_place(own, orders, c, p, half):
    levels = len(own)
    done = orders[half][:p]
    return (
        (c,)
        + tuple(slice(None) if bit in done else own[bit] for bit in range(levels - 1, -1, -1))
        + (half,)
    )


def gather_copy(me, own, orders, mine, out, sems, c, p, half):
    place = gather_place(own, orders, c, p, half)
    return pltpu.make_async_remote_copy(
        src_ref=mine.at[c, half] if p == 0 else out.at[place],
        dst_ref=out.at[place],
        send_sem=sems[0].at[c, p, half],
        recv_sem=sems[1].at[c, p, half],
        device_id={"seq": partner_of(me, orders[half][p])},
        device_id_type=MESH,
    )


def wavefront(chunks, levels):
    return [
        (step, step - p, p)
        for step in range(chunks + levels)
        for p in range(levels, 0, -1)
        if 0 <= step - p < chunks
    ]


def project_kernel(levels, kv, mine, weight, out, held, weights, total, own_sem, send_sem, recv_sem, weight_sem):
    me = lax.axis_index("seq")
    orders = gather_orders(levels)
    own = [bit_of(me, bit) for bit in range(levels)]
    chunks, _, half_rows, width = mine.shape
    depth = weight.shape[0] // kv
    loads = [
        pltpu.make_async_copy(
            weight.at[pl.ds(h * depth, depth)], weights.at[pl.ds(h * depth, depth)], weight_sem.at[h]
        )
        for h in range(kv)
    ]
    greet(me, levels)
    copy = functools.partial(gather_copy, me, own, orders, mine, held, (send_sem, recv_sem))
    own_place = digits_of(me, levels)
    locals_ = [
        pltpu.make_async_copy(mine.at[c], held.at[(c,) + own_place], own_sem.at[c])
        for c in range(chunks)
    ]
    for c in range(chunks):
        for half in range(2):
            copy(c, 0, half).start()
    for one in locals_ + loads:
        one.start()

    kv_levels = kv.bit_length() - 1
    parts = 1 << (levels - kv_levels)
    group = depth // width
    some = 2 * half_rows // group

    def multiply(first, last):
        rows = (last - first) * parts * some
        at = first * parts * some

        def body(h, carry):
            term = None
            for g in range(0, group, 2):
                sides = []
                for i in (g, g + 1):
                    half, start = divmod(i * some, half_rows)
                    pieces = [
                        held[(c,) + digits_of(h, kv_levels) + digits_of(part, levels - kv_levels) + (half, pl.ds(start, some))]
                        for c in range(first, last)
                        for part in range(parts)
                    ]
                    sides.append(jnp.concatenate(pieces, axis=0))
                left = jnp.concatenate(sides, axis=1)
                right = weights[pl.ds(pl.multiple_of(h * depth + g * width, width), 2 * width), :]
                now = jnp.dot(left, right, preferred_element_type=jnp.float32)
                term = now if term is None else term + now
            total[at : at + rows, :] += term
            return carry

        total[at : at + rows, :] = jnp.zeros((rows, total.shape[1]), jnp.float32)
        lax.fori_loop(0, kv, body, 0)
        out[at : at + rows, :] = total[at : at + rows, :].astype(out.dtype)

    for _, c, p in wavefront(chunks, levels):
        if p == 1:
            locals_[c].wait()
        for half in range(2):
            copy(c, p - 1, half).wait_recv()
            if p < levels:
                copy(c, p, half).start()
        if p == levels - 1 and c == chunks - 1:
            for one in loads:
                one.wait()
            multiply(0, chunks - 1)
    multiply(chunks - 1, chunks)
    for c in range(chunks):
        for p in range(levels):
            for half in range(2):
                copy(c, p, half).wait_send()


def gather_project(block, weight, count, kv, collective_id):
    chunks, _, half_rows, width = block.shape
    levels = count.bit_length() - 1
    columns = weight.shape[1]
    rows = chunks * count * 2 * half_rows * width // weight.shape[0]
    return pl.pallas_call(
        functools.partial(project_kernel, levels, kv),
        out_shape=jax.ShapeDtypeStruct((rows, columns), jnp.bfloat16),
        in_specs=[pl.BlockSpec(memory_space=pl.ANY)] * 2,
        out_specs=pl.BlockSpec(memory_space=pltpu.VMEM),
        scratch_shapes=[
            pltpu.VMEM((chunks,) + (2,) * levels + block.shape[1:], block.dtype),
            pltpu.VMEM(weight.shape, weight.dtype),
            pltpu.VMEM((rows, columns), jnp.float32),
            pltpu.SemaphoreType.DMA((chunks,)),
            pltpu.SemaphoreType.DMA((chunks, levels, 2)),
            pltpu.SemaphoreType.DMA((chunks, levels, 2)),
            pltpu.SemaphoreType.DMA((kv,)),
        ],
        compiler_params=pltpu.CompilerParams(
            collective_id=collective_id, has_side_effects=True, vmem_limit_bytes=40 * 2**20
        ),
    )(block, weight)


def attend_kernel(
    scale, levels,
    lengths, mine, k, v, own_bias, out, tree,
    everyone, k_held, v_held, k_wide, v_wide, tree_wide,
    work, work_s, keep, own_sem, send_sem, recv_sem, cache_sem, tree_sem, out_send, out_recv,
    *held_all,
):
    me = lax.axis_index("seq")
    orders = gather_orders(levels)
    backward = tuple(order[::-1] for order in orders)
    own = [bit_of(me, bit) for bit in range(levels)]
    held, held_s = held_all[:levels], held_all[levels:]
    requests, ctx, kv, width = k.shape
    group = (mine.shape[2] - 2 * kv) // kv
    heads = group * kv
    count = 1 << levels
    nodes = 2 * count
    parts = count // kv
    tile = 2 * width
    offset = me * ctx

    copy = functools.partial(gather_copy, me, own, orders, mine, everyone, (send_sem, recv_sem))
    own_place = digits_of(me, levels)
    loads = [
        [
            pltpu.make_async_copy(source.at[r], target.at[r], cache_sem.at[kind, r])
            for kind, (source, target) in enumerate(((k, k_held), (v, v_held)))
        ]
        for r in range(requests)
    ]

    def own_copy(c):
        return pltpu.make_async_copy(mine.at[c], everyone.at[(c,) + own_place], own_sem.at[c])

    def tree_copy(c):
        spread = (slice(None),) * (levels + 1)
        return pltpu.make_async_copy(
            everyone.at[(c,) + spread + (pl.ds(heads, 2 * kv),)], tree.at[c], tree_sem.at[c]
        )

    greet(me, levels)
    for c in range(requests):
        for half in range(2):
            copy(c, 0, half).start()
    for c in range(requests):
        own_copy(c).start()
    for r in range(requests):
        for one in loads[r]:
            one.start()

    def forward(c, p):
        if p == 1:
            own_copy(c).wait()
        for half in range(2):
            copy(c, p - 1, half).wait_recv()
            if p < levels:
                copy(c, p, half).start()
        if p == levels:
            tree_copy(c).start()

    diagonal = lax.broadcasted_iota(jnp.int32, (width, width), 0) == lax.broadcasted_iota(
        jnp.int32, (width, width), 1
    )

    def block(rows, key, value, bias):
        scores = lax.dot_general(
            rows, key, (((1,), (1,)), ((), ())), preferred_element_type=jnp.float32
        )
        scores = scores * (scale * LOG2E) + bias
        top = jnp.max(scores, axis=1, keepdims=True)
        weights = jnp.exp2(scores - top)
        total = jnp.sum(weights, axis=1, keepdims=True)
        number = jnp.dot(weights.astype(jnp.bfloat16), value, preferred_element_type=jnp.float32)
        return top, total, number

    def attention(r, h):
        @pl.when(h == 0)
        def _():
            for kind, (cache, rows, wide) in enumerate(((k, k_held, k_wide), (v, v_held, v_wide))):
                pltpu.make_async_copy(cache.at[r], rows.at[r], cache_sem.at[kind, r]).wait()
                wide[...] = rows[r].astype(jnp.float32).reshape(ctx * kv, width)

        keys = k_wide[pl.ds(h, ctx, stride=kv), :].astype(jnp.bfloat16)
        values = v_wide[pl.ds(h, ctx, stride=kv), :].astype(jnp.bfloat16)
        position = offset + lax.broadcasted_iota(jnp.int32, (1, ctx), 1)
        bias = jnp.where(position < lengths[r], 0.0, NEG)
        everything = (slice(None),) * (levels + 1)

        def queries(part):
            low = levels - (parts.bit_length() - 1)
            where = digits_of(part, levels - low) + (slice(None),) * (low + 1)
            found = everyone[(r,) + where + (pl.ds(pl.multiple_of(h * group, group), group),)]
            return found.reshape(tile, width)

        def store(part, top, total, number):
            number = (number * (1.0 / total)).astype(jnp.bfloat16)
            lines = top + jnp.log2(total)
            place = (r,) + digits_of(h * parts + part, levels)
            for half in range(2):
                span = slice(half * width, (half + 1) * width)
                work[place + (half,)] = number[span]
                work_s[place + (half,)] = jnp.sum(
                    jnp.where(diagonal, lines[span], 0.0), axis=0, keepdims=True
                )

        for part in range(parts):
            store(part, *block(queries(part), keys, values, bias))

        @pl.when(r * kv + h == me)
        def _():
            tree_wide[...] = (
                everyone[(r,) + everything + (pl.ds(heads, 2 * kv),)]
                .astype(jnp.float32)
                .reshape(nodes * 2 * kv, width)
            )
            own_k = tree_wide[pl.ds(h, nodes, stride=2 * kv), :].astype(jnp.bfloat16)
            own_v = tree_wide[pl.ds(kv + h, nodes, stride=2 * kv), :].astype(jnp.bfloat16)
            for part in range(parts):
                rows = queries(part)
                top, total, number = block(rows, keys, values, bias)
                t_top, t_total, t_number = block(
                    rows, own_k, own_v, own_bias[part * tile : (part + 1) * tile]
                )
                high = jnp.maximum(top, t_top)
                fa, fb = jnp.exp2(top - high), jnp.exp2(t_top - high)
                store(part, high, total * fa + t_total * fb, number * fa + t_number * fb)

    def send(c, p, half):
        bit_now = backward[half][p]
        done = backward[half][:p]
        where = tuple(
            own[bit] if bit in done else 1 - own[bit] if bit == bit_now else slice(None)
            for bit in range(levels - 1, -1, -1)
        )
        place = (c,) + where + (half,)
        return [
            pltpu.make_async_remote_copy(
                src_ref=source.at[place],
                dst_ref=target.at[c, half],
                send_sem=out_send.at[kind, c, p, half],
                recv_sem=out_recv.at[kind, c, p, half],
                device_id={"seq": partner_of(me, bit_now)},
                device_id_type=MESH,
            )
            for kind, (source, target) in enumerate(((work, held[p]), (work_s, held_s[p])))
        ]

    def merge(c, p, half):
        order = backward[half]
        done = order[: p + 1]
        last = p == levels - 1

        def one(k, kept):
            fixed = {bit: own[bit] for bit in done}
            if not last:
                fixed[order[p + 1]] = own[order[p + 1]] if kept else 1 - own[order[p + 1]]
            free = [bit for bit in range(levels - 1, -1, -1) if bit not in fixed]
            for rank, bit in enumerate(reversed(free)):
                fixed[bit] = (k // (1 << rank)) % 2
            at_work = (c,) + tuple(fixed[bit] for bit in range(levels - 1, -1, -1)) + (half,)
            at_held = (c, half) + tuple(
                fixed[bit] for bit in range(levels - 1, -1, -1) if bit not in done
            )
            at_keep = (c, half) + tuple(
                fixed[bit] for bit in range(levels - 1, -1, -1) if bit not in order[:2]
            )
            log_a, log_b = work_s[at_work], held_s[p][at_held]
            top = jnp.maximum(log_a, log_b)
            part_a, part_b = jnp.exp2(log_a - top), jnp.exp2(log_b - top)
            total = part_a + part_b
            share = jnp.sum(jnp.where(diagonal, part_a / total, 0.0), axis=1, keepdims=True)
            here = work[at_work].astype(jnp.float32) if p == 0 else keep[at_keep]
            merged = here * share + held[p][at_held].astype(jnp.float32) * (1.0 - share)
            if last:
                out[c, half] = merged.astype(jnp.bfloat16)
                return
            if kept:
                keep[at_keep] = merged
            else:
                work[at_work] = merged.astype(jnp.bfloat16)
            work_s[at_work] = top + jnp.log2(total)

        if last:
            one(0, True)
            return
        for kept in (False, True):
            size = 1 << (levels - 2 - p)
            if size == 1:
                one(0, kept)
            else:
                lax.fori_loop(0, size, lambda k, carry, kept=kept: (one(k, kept), carry)[1], 0)
            if not kept:
                for pending in send(c, p + 1, half):
                    pending.start()

    def reduce(c, p):
        for half in range(2):
            if p == 0:
                for one in send(c, 0, half):
                    one.start()
            else:
                for one in send(c, p - 1, half):
                    one.wait_recv()
                merge(c, p - 1, half)

    events = []
    late = {}
    for step, c, p in wavefront(requests, levels):
        if step <= levels:
            forward(c, p)
        else:
            late.setdefault(step, []).append((c, p))
    for step, found in late.items():
        after = step - levels
        for c, p in found:
            if p == levels:
                slot = c * kv - 1
            else:
                slot = min((after - 1) * kv + (3 if p == levels - 1 else 1), c * kv - 2)
            events.append((slot, 0, -c, functools.partial(forward, c, p)))
    for c in range(requests):
        base = (c + 1) * kv - 1
        for p, wait in enumerate((0, 2, 5, 8, 10, 12)[: levels + 1]):
            events.append((base + wait, 1, -c, functools.partial(reduce, c, p)))
    events.sort(key=lambda e: e[:3])
    total_steps = requests * kv

    def step_body(i, carry):
        attention(i // kv, i % kv)
        for slot, _, _, act in events:
            if slot < total_steps:
                pl.when(i == slot)(act)
        return carry

    lax.fori_loop(0, total_steps, step_body, 0)
    for slot, _, _, act in events:
        if slot >= total_steps:
            act()
    for c in range(requests):
        tree_copy(c).wait()
        for p in range(levels):
            for half in range(2):
                copy(c, p, half).wait_send()
                for one in send(c, p, half):
                    one.wait_send()


def attend(scale, count, lengths, mine, k, v, own_bias, collective_id):
    requests, ctx, kv, width = k.shape
    levels = count.bit_length() - 1
    bits = (2,) * levels
    rows = 2 * mine.shape[2] - 4 * kv
    half_rows = rows // 2
    work = requests * kv * own_bias.shape[0] * ctx
    hbm = pl.BlockSpec(memory_space=pl.ANY)
    vmem = pl.BlockSpec(memory_space=pltpu.VMEM)
    held = [
        pltpu.VMEM((requests, 2) + bits[: levels - 1 - p] + (half_rows, width), jnp.bfloat16)
        for p in range(levels)
    ]
    held_s = [
        pltpu.VMEM((requests, 2) + bits[: levels - 1 - p] + (1, half_rows), jnp.float32)
        for p in range(levels)
    ]
    return pl.pallas_call(
        functools.partial(attend_kernel, scale, levels),
        in_specs=[pl.BlockSpec(memory_space=pltpu.SMEM), hbm, hbm, hbm, vmem],
        out_specs=[vmem, hbm],
        out_shape=[
            jax.ShapeDtypeStruct((requests, 2, half_rows, width), jnp.bfloat16),
            jax.ShapeDtypeStruct((requests,) + bits + (2, 2 * kv, width), mine.dtype),
        ],
        scratch_shapes=[
            pltpu.VMEM((requests,) + bits + mine.shape[1:], mine.dtype),
            pltpu.VMEM(k.shape, k.dtype),
            pltpu.VMEM(v.shape, v.dtype),
            pltpu.VMEM((ctx * kv, width), jnp.float32),
            pltpu.VMEM((ctx * kv, width), jnp.float32),
            pltpu.VMEM((2 * count * 2 * kv, width), jnp.float32),
            pltpu.VMEM((requests,) + bits + (2, half_rows, width), jnp.bfloat16),
            pltpu.VMEM((requests,) + bits + (2, 1, half_rows), jnp.float32),
            pltpu.VMEM((requests, 2) + bits[2:] + (half_rows, width), jnp.float32),
            pltpu.SemaphoreType.DMA((requests,)),
            pltpu.SemaphoreType.DMA((requests, levels, 2)),
            pltpu.SemaphoreType.DMA((requests, levels, 2)),
            pltpu.SemaphoreType.DMA((2, requests)),
            pltpu.SemaphoreType.DMA((requests,)),
            pltpu.SemaphoreType.DMA((2, requests, levels, 2)),
            pltpu.SemaphoreType.DMA((2, requests, levels, 2)),
        ]
        + held
        + held_s,
        compiler_params=pltpu.CompilerParams(
            collective_id=collective_id, has_side_effects=True, vmem_limit_bytes=60 * 2**20
        ),
        cost_estimate=pl.CostEstimate(
            flops=4 * work * width, bytes_accessed=4 * k.size * 2, transcendentals=work
        ),
    )(lengths, mine, k, v, own_bias)


def append_kernel(where, lengths, accepted, count, k, v, tree, k_out, v_out):
    r = pl.program_id(0)
    ctx, kv = k.shape[1:3]
    for kind, (cache, target) in enumerate(((k, k_out), (v, v_out))):
        target[...] = cache[...]
        for j in range(accepted.shape[1]):
            slot = lengths[r] + j - where[0]

            @pl.when((j < count[r]) & (slot >= 0) & (slot < ctx))
            def _():
                target[0, slot] = tree[0, accepted[r, j], kind]


def append(where, lengths, accepted, count, k, v, tree):
    requests, ctx, kv, width = k.shape
    cache = pl.BlockSpec((1, ctx, kv, width), lambda r, *_: (r, 0, 0, 0))
    return pl.pallas_call(
        append_kernel,
        grid_spec=pltpu.PrefetchScalarGridSpec(
            num_scalar_prefetch=4,
            grid=(requests,),
            in_specs=[
                cache, cache,
                pl.BlockSpec((1,) + tree.shape[1:], lambda r, *_: (r, 0, 0, 0, 0)),
            ],
            out_specs=[cache, cache],
        ),
        out_shape=[jax.ShapeDtypeStruct(k.shape, k.dtype)] * 2,
        compiler_params=pltpu.CompilerParams(vmem_limit_bytes=24 * 2**20),
    )(where, lengths, accepted, count, k, v, tree)


def on_device(
    tree_queries,
    tree_keys,
    tree_values,
    cache_keys,
    cache_values,
    out_weight,
    context_lengths,
    parents,
    accepted_nodes,
    accepted_count,
):
    requests, ctx, kv, width = cache_keys.shape
    node_local, heads = tree_queries.shape[1:3]
    group = heads // kv
    count = lax.axis_size("seq")
    nodes = node_local * count
    part = kv * nodes // count
    me = lax.axis_index("seq")
    sent = jnp.concatenate([tree_queries, tree_keys, tree_values], axis=2)
    own_request = lax.rem(me, requests * kv) // kv
    own_reach = lax.dynamic_index_in_dim(ancestors(parents), own_request, 0, keepdims=False)
    own_bias = jnp.repeat(jnp.where(own_reach > 0.5, 0.0, NEG), group, axis=0)
    home, tree = attend(
        1.0 / math.sqrt(width), count, context_lengths, sent, cache_keys, cache_values, own_bias, 1
    )
    home = home.reshape(requests, part, group, width).swapaxes(1, 2)
    projected = gather_project(
        home.reshape(requests, 2, part * group // 2, width), out_weight, count, kv, 2
    )
    keys_out, values_out = append(
        (me * ctx).astype(jnp.int32).reshape(1),
        context_lengths, accepted_nodes, accepted_count, cache_keys, cache_values,
        tree.reshape(requests, nodes, 2, kv, width),
    )
    return (projected, keys_out, values_out)


def fits(mesh, args):
    queries, keys = args[0], args[3]
    count, split = mesh.shape["seq"], mesh.shape["head"]
    requests, nodes, heads, width = queries.shape
    kv = keys.shape[2]
    rows = nodes * heads // count
    return (
        split == 1
        and count >= 8
        and count & (count - 1) == 0
        and count % kv == 0
        and count >= requests * kv
        and nodes * kv // count % 16 == 0
        and nodes == 2 * count
        and rows == 2 * width
    )


def solution(mesh):
    in_specs = (
        P(None, "seq", "head", None),
        P(None, "seq", "head", None),
        P(None, "seq", "head", None),
        P(None, "seq", "head", None),
        P(None, "seq", "head", None),
        P("head", "seq"),
        P(),
        P(),
        P(),
        P(),
    )
    out_specs = (P("head", "seq"), P(None, "seq", "head", None), P(None, "seq", "head", None))

    def run(*args):
        body = on_device if fits(mesh, args) else on_device_plain
        return jax.shard_map(
            body, mesh=mesh, in_specs=in_specs, out_specs=out_specs, check_vma=False
        )(*args)

    return run
```

```python
import functools
import math

import jax
import jax.numpy as jnp
from jax import lax
from jax.experimental import pallas as pl
from jax.experimental.pallas import tpu as pltpu
from jax.sharding import PartitionSpec as P

NEG = -1e30


def ancestors(parents):
    count_nodes = parents.shape[1]
    columns = jnp.arange(count_nodes, dtype=jnp.int32)
    linked = (parents[:, :, None] == columns[None, None, :]) | (
        columns[:, None] == columns[None, :]
    )[None]
    closure = linked.astype(jnp.float32)
    for rounds in range(max(count_nodes - 1, 1).bit_length()):
        closure = jnp.minimum(jnp.matmul(closure, closure, precision=lax.Precision.HIGHEST), 1.0)
    return closure


def partial_attention(queries, keys, values, allowed, scale_factor):
    scores = (
        jnp.einsum("rnhge,rphe->rnhgp", queries, keys, preferred_element_type=jnp.float32)
        * scale_factor
    )
    row_top = jnp.max(jnp.where(allowed, scores, NEG), axis=-1)
    weights = jnp.where(allowed, jnp.exp(scores - row_top[..., None]), 0.0)
    row_sum = jnp.sum(weights, axis=-1)
    numerator = jnp.einsum(
        "rnhgp,rphe->rnhge",
        weights.astype(jnp.bfloat16),
        values,
        preferred_element_type=jnp.float32,
    )
    return (row_top, row_sum, numerator)


def merge_parts(first, second):
    top_first, sum_first, acc_first = first
    top_second, sum_second, acc_second = second
    row_top = jnp.maximum(top_first, top_second)
    scale_first = jnp.exp(top_first - row_top)
    scale_second = jnp.exp(top_second - row_top)
    row_sum = sum_first * scale_first + sum_second * scale_second
    numerator = acc_first * scale_first[..., None] + acc_second * scale_second[..., None]
    return (row_top, row_sum, numerator)


def append_rows(cache_block, tree_all, choose, slot_map, written):
    picked = jnp.einsum(
        "rjn,rnhe->rjhe", choose, tree_all, preferred_element_type=jnp.float32
    ).astype(jnp.bfloat16)
    placed = jnp.einsum(
        "rjp,rjhe->rphe", slot_map, picked, preferred_element_type=jnp.float32
    ).astype(jnp.bfloat16)
    return jnp.where(written[:, :, None, None], placed, cache_block)


def on_device_plain(
    tree_queries,
    tree_keys,
    tree_values,
    cache_keys,
    cache_values,
    out_weight,
    context_lengths,
    parents,
    accepted_nodes,
    accepted_count,
):
    requests, ctx_local, kv_local, head_dim = cache_keys.shape
    node_local, q_local = (tree_queries.shape[1], tree_queries.shape[2])
    group_size = q_local // kv_local
    path_len = accepted_nodes.shape[1]
    scale_factor = 1.0 / math.sqrt(head_dim)
    seq_index = lax.axis_index("seq")
    seq_count = lax.axis_size("seq")
    nodes_all = node_local * seq_count
    offset = seq_index * ctx_local
    grouped = tree_queries.reshape(requests, node_local, kv_local, group_size, head_dim)
    tree_all_k, tree_all_v = (
        lax.all_gather(tree_keys, "seq", axis=1, tiled=True),
        lax.all_gather(tree_values, "seq", axis=1, tiled=True),
    )
    closure = ancestors(parents)
    home_rows = lax.dynamic_slice_in_dim(closure, seq_index * node_local, node_local, 1)
    tree_state = partial_attention(
        grouped, tree_all_k, tree_all_v, home_rows[:, :, None, None, :] > 0.5, scale_factor
    )
    positions = offset + jnp.arange(ctx_local, dtype=jnp.int32)
    usable = (positions[None, :] < context_lengths[:, None])[:, None, None, None, :]
    everyone = lax.all_gather(grouped, "seq", axis=1, tiled=True)
    row_top, row_sum, numerator = partial_attention(
        everyone, cache_keys, cache_values, usable, scale_factor
    )
    highest = lax.pmax(row_top, "seq")
    factor = jnp.exp(row_top - highest)
    summed_acc, summed_sum = (
        lax.psum_scatter(numerator * factor[..., None], "seq", scatter_dimension=1, tiled=True),
        lax.psum_scatter(row_sum * factor, "seq", scatter_dimension=1, tiled=True),
    )
    home_top = lax.dynamic_slice_in_dim(highest, seq_index * node_local, node_local, 1)
    cache_state = (home_top, summed_sum, summed_acc)
    final_top, final_sum, final_acc = merge_parts(cache_state, tree_state)
    attention = (
        (final_acc / final_sum[..., None])
        .astype(jnp.bfloat16)
        .reshape(requests, node_local, q_local * head_dim)
    )
    partial_terms = jnp.einsum(
        "rnx,xd->rnd",
        lax.all_gather(attention, "seq", axis=1, tiled=True),
        out_weight,
        preferred_element_type=jnp.float32,
    )
    partial_terms = partial_terms.reshape(requests * nodes_all, out_weight.shape[1])
    projected = lax.psum_scatter(partial_terms, "head", scatter_dimension=0, tiled=True).astype(
        jnp.bfloat16
    )
    choose = (
        accepted_nodes[:, :, None] == jnp.arange(nodes_all, dtype=jnp.int32)[None, None, :]
    ).astype(jnp.bfloat16)
    steps_index = jnp.arange(path_len, dtype=jnp.int32)
    targets = context_lengths[:, None] + steps_index[None, :] - offset
    alive = steps_index[None, :] < accepted_count[:, None]
    slot_flags = (
        targets[:, :, None] == jnp.arange(ctx_local, dtype=jnp.int32)[None, None, :]
    ) & alive[:, :, None]
    slot_map = slot_flags.astype(jnp.bfloat16)
    written = jnp.sum(slot_flags.astype(jnp.float32), axis=1) > 0.5
    keys_out = append_rows(cache_keys, tree_all_k, choose, slot_map, written)
    values_out = append_rows(cache_values, tree_all_v, choose, slot_map, written)
    return (projected, keys_out, values_out)


MESH = pl.DeviceIdType.MESH
LOG2E = math.log2(math.e)


def bit_of(me, bit):
    return (me // (1 << bit)) % 2


def partner_of(me, bit):
    return me + (1 - 2 * bit_of(me, bit)) * (1 << bit)


def greet(me, levels):
    barrier = pltpu.get_barrier_semaphore()
    for bit in range(levels):
        pl.semaphore_signal(
            barrier, inc=1, device_id={"seq": partner_of(me, bit)}, device_id_type=MESH
        )
    pl.semaphore_wait(barrier, levels)


def gather_orders(levels):
    high = list(range(levels - 1, 2, -1))
    return (high + [1, 2, 0], high + [2, 1, 0])


def digits_of(value, levels):
    return tuple((value // (1 << bit)) % 2 for bit in range(levels - 1, -1, -1))


def gather_place(own, orders, c, p, half):
    levels = len(own)
    done = orders[half][:p]
    return (
        (c,)
        + tuple(slice(None) if bit in done else own[bit] for bit in range(levels - 1, -1, -1))
        + (half,)
    )


def gather_copy(me, own, orders, mine, out, sems, c, p, half):
    place = gather_place(own, orders, c, p, half)
    return pltpu.make_async_remote_copy(
        src_ref=mine.at[c, half] if p == 0 else out.at[place],
        dst_ref=out.at[place],
        send_sem=sems[0].at[c, p, half],
        recv_sem=sems[1].at[c, p, half],
        device_id={"seq": partner_of(me, orders[half][p])},
        device_id_type=MESH,
    )


def wavefront(chunks, levels):
    return [
        (step, step - p, p)
        for step in range(chunks + levels)
        for p in range(levels, 0, -1)
        if 0 <= step - p < chunks
    ]


def project_kernel(levels, kv, cuts, mine, weight, out, held, weights, total, own_sem, send_sem, recv_sem, weight_sem):
    me = lax.axis_index("seq")
    orders = gather_orders(levels)
    own = [bit_of(me, bit) for bit in range(levels)]
    chunks, _, half_rows, width = mine.shape
    depth = weight.shape[0] // kv
    loads = [
        pltpu.make_async_copy(
            weight.at[pl.ds(h * depth, depth)], weights.at[pl.ds(h * depth, depth)], weight_sem.at[h]
        )
        for h in range(kv)
    ]
    greet(me, levels)
    copy = functools.partial(gather_copy, me, own, orders, mine, held, (send_sem, recv_sem))
    own_place = digits_of(me, levels)
    locals_ = [
        pltpu.make_async_copy(mine.at[c], held.at[(c,) + own_place], own_sem.at[c])
        for c in range(chunks)
    ]

    def begin(c):
        if c < chunks:
            for half in range(2):
                copy(c, 0, half).start()

    begin(0)
    begin(1)
    for one in locals_ + loads:
        one.start()

    kv_levels = kv.bit_length() - 1
    parts = 1 << (levels - kv_levels)
    group = depth // width
    requests = chunks // cuts
    some = cuts * 2 * half_rows // group

    def multiply(first, last):
        rows = (last - first) * parts * some
        at = first * parts * some

        def body(h, carry):
            term = None
            for g in range(0, group, 2):
                sides = []
                for i in (g, g + 1):
                    cut, start = divmod(i * some, 2 * half_rows)
                    half, start = divmod(start, half_rows)
                    pieces = [
                        held[(r * cuts + cut,) + digits_of(h, kv_levels) + digits_of(part, levels - kv_levels) + (half, pl.ds(start, some))]
                        for r in range(first, last)
                        for part in range(parts)
                    ]
                    sides.append(jnp.concatenate(pieces, axis=0))
                left = jnp.concatenate(sides, axis=1)
                right = weights[pl.ds(pl.multiple_of(h * depth + g * width, width), 2 * width), :]
                now = jnp.dot(left, right, preferred_element_type=jnp.float32)
                term = now if term is None else term + now
            total[at : at + rows, :] += term
            return carry

        total[at : at + rows, :] = jnp.zeros((rows, total.shape[1]), jnp.float32)
        lax.fori_loop(0, kv, body, 0)
        out[at : at + rows, :] = total[at : at + rows, :].astype(out.dtype)

    for _, c, p in wavefront(chunks, levels):
        if p == 1:
            locals_[c].wait()
        for half in range(2):
            copy(c, p - 1, half).wait_recv()
            if p < levels:
                copy(c, p, half).start()
        if p == 1:
            begin(c + 2)
        if p == levels - 1 and c == chunks - 1:
            for one in loads:
                one.wait()
            multiply(0, requests - 1)
    multiply(requests - 1, requests)
    for c in range(chunks):
        for p in range(levels):
            for half in range(2):
                copy(c, p, half).wait_send()


def gather_project(block, weight, count, kv, cuts, collective_id):
    chunks, _, half_rows, width = block.shape
    levels = count.bit_length() - 1
    columns = weight.shape[1]
    rows = chunks * count * 2 * half_rows * width // weight.shape[0]
    return pl.pallas_call(
        functools.partial(project_kernel, levels, kv, cuts),
        out_shape=jax.ShapeDtypeStruct((rows, columns), jnp.bfloat16),
        in_specs=[pl.BlockSpec(memory_space=pl.ANY)] * 2,
        out_specs=pl.BlockSpec(memory_space=pltpu.VMEM),
        scratch_shapes=[
            pltpu.VMEM((chunks,) + (2,) * levels + block.shape[1:], block.dtype),
            pltpu.VMEM(weight.shape, weight.dtype),
            pltpu.VMEM((rows, columns), jnp.float32),
            pltpu.SemaphoreType.DMA((chunks,)),
            pltpu.SemaphoreType.DMA((chunks, levels, 2)),
            pltpu.SemaphoreType.DMA((chunks, levels, 2)),
            pltpu.SemaphoreType.DMA((kv,)),
        ],
        compiler_params=pltpu.CompilerParams(
            collective_id=collective_id, has_side_effects=True, vmem_limit_bytes=40 * 2**20
        ),
    )(block, weight)


def attend_kernel(
    scale, levels,
    lengths, mine, k, v, own_bias, out, tree,
    everyone, k_held, v_held, k_wide, v_wide, tree_wide,
    work, work_s, keep, own_sem, send_sem, recv_sem, cache_sem, tree_sem, out_send, out_recv,
    *held_all,
):
    me = lax.axis_index("seq")
    orders = gather_orders(levels)
    backward = tuple(order[::-1] for order in orders)
    own = [bit_of(me, bit) for bit in range(levels)]
    held, held_s = held_all[:levels], held_all[levels:]
    requests, ctx, kv, width = k.shape
    group = (mine.shape[2] - 2 * kv) // kv
    heads = group * kv
    count = 1 << levels
    nodes = 2 * count
    parts = count // kv
    tile = 2 * width
    offset = me * ctx

    copy = functools.partial(gather_copy, me, own, orders, mine, everyone, (send_sem, recv_sem))
    own_place = digits_of(me, levels)
    loads = [
        [
            pltpu.make_async_copy(source.at[r], target.at[r], cache_sem.at[kind, r])
            for kind, (source, target) in enumerate(((k, k_held), (v, v_held)))
        ]
        for r in range(requests)
    ]

    def own_copy(c):
        return pltpu.make_async_copy(mine.at[c], everyone.at[(c,) + own_place], own_sem.at[c])

    def tree_copy(c):
        spread = (slice(None),) * (levels + 1)
        return pltpu.make_async_copy(
            everyone.at[(c,) + spread + (pl.ds(heads, 2 * kv),)], tree.at[c], tree_sem.at[c]
        )

    greet(me, levels)

    def begin(c):
        if c < requests:
            for half in range(2):
                copy(c, 0, half).start()

    begin(0)
    begin(1)
    for c in range(requests):
        own_copy(c).start()
    for r in range(requests):
        for one in loads[r]:
            one.start()

    def forward(c, p):
        if p == 1:
            own_copy(c).wait()
        for half in range(2):
            copy(c, p - 1, half).wait_recv()
            if p < levels:
                copy(c, p, half).start()
        if p == levels:
            tree_copy(c).start()

    diagonal = lax.broadcasted_iota(jnp.int32, (width, width), 0) == lax.broadcasted_iota(
        jnp.int32, (width, width), 1
    )

    def score(rows, key):
        return lax.dot_general(
            rows, key, (((1,), (1,)), ((), ())), preferred_element_type=jnp.float32
        )

    def block(scores, value, bias):
        scores = scores * (scale * LOG2E) + bias
        top = jnp.max(scores, axis=1, keepdims=True)
        weights = jnp.exp2(scores - top)
        total = jnp.sum(weights, axis=1, keepdims=True)
        number = jnp.dot(weights.astype(jnp.bfloat16), value, preferred_element_type=jnp.float32)
        return top, total, number

    def attention(r, h):
        @pl.when(h == 0)
        def _():
            for kind, (cache, rows, wide) in enumerate(((k, k_held, k_wide), (v, v_held, v_wide))):
                pltpu.make_async_copy(cache.at[r], rows.at[r], cache_sem.at[kind, r]).wait()
                wide[...] = rows[r].astype(jnp.float32).reshape(ctx * kv, width)

        keys = k_wide[pl.ds(h, ctx, stride=kv), :].astype(jnp.bfloat16)
        values = v_wide[pl.ds(h, ctx, stride=kv), :].astype(jnp.bfloat16)
        position = offset + lax.broadcasted_iota(jnp.int32, (1, ctx), 1)
        bias = jnp.where(position < lengths[r], 0.0, NEG)
        everything = (slice(None),) * (levels + 1)

        def queries(part):
            low = levels - (parts.bit_length() - 1)
            where = digits_of(part, levels - low) + (slice(None),) * (low + 1)
            found = everyone[(r,) + where + (pl.ds(pl.multiple_of(h * group, group), group),)]
            return found.reshape(tile, width)

        def store(part, top, total, number):
            number = (number * (1.0 / total)).astype(jnp.bfloat16)
            lines = top + jnp.log2(total)
            place = (r,) + digits_of(h * parts + part, levels)
            for half in range(2):
                span = slice(half * width, (half + 1) * width)
                work[place + (half,)] = number[span]
                work_s[place + (half,)] = jnp.sum(
                    jnp.where(diagonal, lines[span], 0.0), axis=0, keepdims=True
                )

        ahead = score(queries(0), keys)
        for part in range(parts):
            scores = ahead
            if part + 1 < parts:
                ahead = score(queries(part + 1), keys)
            store(part, *block(scores, values, bias))

        @pl.when(r * kv + h == me)
        def _():
            tree_wide[...] = (
                everyone[(r,) + everything + (pl.ds(heads, 2 * kv),)]
                .astype(jnp.float32)
                .reshape(nodes * 2 * kv, width)
            )
            own_k = tree_wide[pl.ds(h, nodes, stride=2 * kv), :].astype(jnp.bfloat16)
            own_v = tree_wide[pl.ds(kv + h, nodes, stride=2 * kv), :].astype(jnp.bfloat16)
            for part in range(parts):
                rows = queries(part)
                top, total, number = block(score(rows, keys), values, bias)
                t_top, t_total, t_number = block(
                    score(rows, own_k), own_v, own_bias[part * tile : (part + 1) * tile]
                )
                high = jnp.maximum(top, t_top)
                fa, fb = jnp.exp2(top - high), jnp.exp2(t_top - high)
                store(part, high, total * fa + t_total * fb, number * fa + t_number * fb)

    def send(c, p, half):
        bit_now = backward[half][p]
        done = backward[half][:p]
        where = tuple(
            own[bit] if bit in done else 1 - own[bit] if bit == bit_now else slice(None)
            for bit in range(levels - 1, -1, -1)
        )
        place = (c,) + where + (half,)
        return [
            pltpu.make_async_remote_copy(
                src_ref=source.at[place],
                dst_ref=target.at[c, half],
                send_sem=out_send.at[kind, c, p, half],
                recv_sem=out_recv.at[kind, c, p, half],
                device_id={"seq": partner_of(me, bit_now)},
                device_id_type=MESH,
            )
            for kind, (source, target) in enumerate(((work, held[p]), (work_s, held_s[p])))
        ]

    def merge(c, p, half):
        order = backward[half]
        done = order[: p + 1]
        last = p == levels - 1

        def one(k, kept):
            fixed = {bit: own[bit] for bit in done}
            if not last:
                fixed[order[p + 1]] = own[order[p + 1]] if kept else 1 - own[order[p + 1]]
            free = [bit for bit in range(levels - 1, -1, -1) if bit not in fixed]
            for rank, bit in enumerate(reversed(free)):
                fixed[bit] = (k // (1 << rank)) % 2
            at_work = (c,) + tuple(fixed[bit] for bit in range(levels - 1, -1, -1)) + (half,)
            at_held = (c, half) + tuple(
                fixed[bit] for bit in range(levels - 1, -1, -1) if bit not in done
            )
            at_keep = (c, half) + tuple(
                fixed[bit] for bit in range(levels - 1, -1, -1) if bit not in order[:2]
            )
            log_a, log_b = work_s[at_work], held_s[p][at_held]
            top = jnp.maximum(log_a, log_b)
            part_a, part_b = jnp.exp2(log_a - top), jnp.exp2(log_b - top)
            total = part_a + part_b
            share = jnp.sum(jnp.where(diagonal, part_a / total, 0.0), axis=1, keepdims=True)
            here = work[at_work].astype(jnp.float32) if p == 0 else keep[at_keep]
            merged = here * share + held[p][at_held].astype(jnp.float32) * (1.0 - share)
            if last:
                out[c, half] = merged.astype(jnp.bfloat16)
                return
            if kept:
                keep[at_keep] = merged
            else:
                work[at_work] = merged.astype(jnp.bfloat16)
            work_s[at_work] = top + jnp.log2(total)

        if last:
            one(0, True)
            return
        for kept in (False, True):
            size = 1 << (levels - 2 - p)
            if size == 1:
                one(0, kept)
            else:
                lax.fori_loop(0, size, lambda k, carry, kept=kept: (one(k, kept), carry)[1], 0)
            if not kept:
                for pending in send(c, p + 1, half):
                    pending.start()

    def reduce(c, p):
        for half in range(2):
            if p == 0:
                for one in send(c, 0, half):
                    one.start()
            else:
                for one in send(c, p - 1, half):
                    one.wait_recv()
                merge(c, p - 1, half)

    events = []
    late = {}
    for step, c, p in wavefront(requests, levels):
        if step <= levels:
            forward(c, p)
            if p == 1:
                begin(step + 1)
        else:
            late.setdefault(step, []).append((c, p))
    for step, found in late.items():
        after = step - levels
        for c, p in found:
            if p == levels:
                slot = c * kv - 1
            else:
                slot = min((after - 1) * kv + (3 if p == levels - 1 else 1), c * kv - 2)
            events.append((slot, 0, -c, functools.partial(forward, c, p)))
    for c in range(requests):
        base = (c + 1) * kv - 1
        for p, wait in enumerate((0, 2, 7, 11, 13, 15)[: levels + 1]):
            events.append((base + wait, 1, -c, functools.partial(reduce, c, p)))
    events.sort(key=lambda e: e[:3])
    total_steps = requests * kv

    def step_body(i, carry):
        attention(i // kv, i % kv)
        for slot, _, _, act in events:
            if slot < total_steps:
                pl.when(i == slot)(act)
        return carry

    lax.fori_loop(0, total_steps, step_body, 0)
    for slot, _, _, act in events:
        if slot >= total_steps:
            act()
    for c in range(requests):
        tree_copy(c).wait()
        for p in range(levels):
            for half in range(2):
                copy(c, p, half).wait_send()
                for one in send(c, p, half):
                    one.wait_send()


def attend(scale, count, lengths, mine, k, v, own_bias, collective_id):
    requests, ctx, kv, width = k.shape
    levels = count.bit_length() - 1
    bits = (2,) * levels
    rows = 2 * mine.shape[2] - 4 * kv
    half_rows = rows // 2
    work = requests * kv * own_bias.shape[0] * ctx
    hbm = pl.BlockSpec(memory_space=pl.ANY)
    vmem = pl.BlockSpec(memory_space=pltpu.VMEM)
    held = [
        pltpu.VMEM((requests, 2) + bits[: levels - 1 - p] + (half_rows, width), jnp.bfloat16)
        for p in range(levels)
    ]
    held_s = [
        pltpu.VMEM((requests, 2) + bits[: levels - 1 - p] + (1, half_rows), jnp.float32)
        for p in range(levels)
    ]
    return pl.pallas_call(
        functools.partial(attend_kernel, scale, levels),
        in_specs=[pl.BlockSpec(memory_space=pltpu.SMEM), hbm, hbm, hbm, vmem],
        out_specs=[vmem, hbm],
        out_shape=[
            jax.ShapeDtypeStruct((requests, 2, half_rows, width), jnp.bfloat16),
            jax.ShapeDtypeStruct((requests,) + bits + (2, 2 * kv, width), mine.dtype),
        ],
        scratch_shapes=[
            pltpu.VMEM((requests,) + bits + mine.shape[1:], mine.dtype),
            pltpu.VMEM(k.shape, k.dtype),
            pltpu.VMEM(v.shape, v.dtype),
            pltpu.VMEM((ctx * kv, width), jnp.float32),
            pltpu.VMEM((ctx * kv, width), jnp.float32),
            pltpu.VMEM((2 * count * 2 * kv, width), jnp.float32),
            pltpu.VMEM((requests,) + bits + (2, half_rows, width), jnp.bfloat16),
            pltpu.VMEM((requests,) + bits + (2, 1, half_rows), jnp.float32),
            pltpu.VMEM((requests, 2) + bits[2:] + (half_rows, width), jnp.float32),
            pltpu.SemaphoreType.DMA((requests,)),
            pltpu.SemaphoreType.DMA((requests, levels, 2)),
            pltpu.SemaphoreType.DMA((requests, levels, 2)),
            pltpu.SemaphoreType.DMA((2, requests)),
            pltpu.SemaphoreType.DMA((requests,)),
            pltpu.SemaphoreType.DMA((2, requests, levels, 2)),
            pltpu.SemaphoreType.DMA((2, requests, levels, 2)),
        ]
        + held
        + held_s,
        compiler_params=pltpu.CompilerParams(
            collective_id=collective_id, has_side_effects=True, vmem_limit_bytes=60 * 2**20
        ),
        cost_estimate=pl.CostEstimate(
            flops=4 * work * width, bytes_accessed=4 * k.size * 2, transcendentals=work
        ),
    )(lengths, mine, k, v, own_bias)


def append_kernel(where, lengths, accepted, count, k, v, tree, k_out, v_out):
    r = pl.program_id(0)
    ctx, kv = k.shape[1:3]
    for kind, (cache, target) in enumerate(((k, k_out), (v, v_out))):
        target[...] = cache[...]
        for j in range(accepted.shape[1]):
            slot = lengths[r] + j - where[0]

            @pl.when((j < count[r]) & (slot >= 0) & (slot < ctx))
            def _():
                target[0, slot] = tree[0, accepted[r, j], kind]


def append(where, lengths, accepted, count, k, v, tree):
    requests, ctx, kv, width = k.shape
    cache = pl.BlockSpec((1, ctx, kv, width), lambda r, *_: (r, 0, 0, 0))
    return pl.pallas_call(
        append_kernel,
        grid_spec=pltpu.PrefetchScalarGridSpec(
            num_scalar_prefetch=4,
            grid=(requests,),
            in_specs=[
                cache, cache,
                pl.BlockSpec((1,) + tree.shape[1:], lambda r, *_: (r, 0, 0, 0, 0)),
            ],
            out_specs=[cache, cache],
        ),
        out_shape=[jax.ShapeDtypeStruct(k.shape, k.dtype)] * 2,
        compiler_params=pltpu.CompilerParams(vmem_limit_bytes=60 * 2**20),
    )(where, lengths, accepted, count, k, v, tree)


def on_device(
    tree_queries,
    tree_keys,
    tree_values,
    cache_keys,
    cache_values,
    out_weight,
    context_lengths,
    parents,
    accepted_nodes,
    accepted_count,
):
    requests, ctx, kv, width = cache_keys.shape
    node_local, heads = tree_queries.shape[1:3]
    group = heads // kv
    count = lax.axis_size("seq")
    nodes = node_local * count
    part = kv * nodes // count
    me = lax.axis_index("seq")
    sent = jnp.concatenate([tree_queries, tree_keys, tree_values], axis=2)
    own_request = lax.rem(me, requests * kv) // kv
    own_reach = lax.dynamic_index_in_dim(ancestors(parents), own_request, 0, keepdims=False)
    own_bias = jnp.repeat(jnp.where(own_reach > 0.5, 0.0, NEG), group, axis=0)
    home, tree = attend(
        1.0 / math.sqrt(width), count, context_lengths, sent, cache_keys, cache_values, own_bias, 1
    )
    home = home.reshape(requests, part, group, width).swapaxes(1, 2)
    cuts = 2
    projected = gather_project(
        home.reshape(requests * cuts, 2, part * group // (2 * cuts), width),
        out_weight, count, kv, cuts, 2,
    )
    keys_out, values_out = append(
        (me * ctx).astype(jnp.int32).reshape(1),
        context_lengths, accepted_nodes, accepted_count, cache_keys, cache_values,
        tree.reshape(requests, nodes, 2, kv, width),
    )
    return (projected, keys_out, values_out)


def fits(mesh, args):
    queries, keys = args[0], args[3]
    count, split = mesh.shape["seq"], mesh.shape["head"]
    requests, nodes, heads, width = queries.shape
    kv = keys.shape[2]
    rows = nodes * heads // count
    return (
        split == 1
        and count >= 8
        and count & (count - 1) == 0
        and count % kv == 0
        and count >= requests * kv
        and nodes * kv // count % 16 == 0
        and nodes == 2 * count
        and rows == 2 * width
    )


def solution(mesh):
    in_specs = (
        P(None, "seq", "head", None),
        P(None, "seq", "head", None),
        P(None, "seq", "head", None),
        P(None, "seq", "head", None),
        P(None, "seq", "head", None),
        P("head", "seq"),
        P(),
        P(),
        P(),
        P(),
    )
    out_specs = (P("head", "seq"), P(None, "seq", "head", None), P(None, "seq", "head", None))

    def run(*args):
        body = on_device if fits(mesh, args) else on_device_plain
        return jax.shard_map(
            body, mesh=mesh, in_specs=in_specs, out_specs=out_specs, check_vma=False
        )(*args)

    return run
```

```python
import functools
import math

import jax
import jax.numpy as jnp
from jax import lax
from jax.experimental import pallas as pl
from jax.experimental.pallas import tpu as pltpu
from jax.sharding import PartitionSpec as P

NEG = -1e30


def ancestors(parents):
    count_nodes = parents.shape[1]
    columns = jnp.arange(count_nodes, dtype=jnp.int32)
    linked = (parents[:, :, None] == columns[None, None, :]) | (
        columns[:, None] == columns[None, :]
    )[None]
    closure = linked.astype(jnp.float32)
    for rounds in range(max(count_nodes - 1, 1).bit_length()):
        closure = jnp.minimum(jnp.matmul(closure, closure, precision=lax.Precision.HIGHEST), 1.0)
    return closure


def partial_attention(queries, keys, values, allowed, scale_factor):
    scores = (
        jnp.einsum("rnhge,rphe->rnhgp", queries, keys, preferred_element_type=jnp.float32)
        * scale_factor
    )
    row_top = jnp.max(jnp.where(allowed, scores, NEG), axis=-1)
    weights = jnp.where(allowed, jnp.exp(scores - row_top[..., None]), 0.0)
    row_sum = jnp.sum(weights, axis=-1)
    numerator = jnp.einsum(
        "rnhgp,rphe->rnhge",
        weights.astype(jnp.bfloat16),
        values,
        preferred_element_type=jnp.float32,
    )
    return (row_top, row_sum, numerator)


def merge_parts(first, second):
    top_first, sum_first, acc_first = first
    top_second, sum_second, acc_second = second
    row_top = jnp.maximum(top_first, top_second)
    scale_first = jnp.exp(top_first - row_top)
    scale_second = jnp.exp(top_second - row_top)
    row_sum = sum_first * scale_first + sum_second * scale_second
    numerator = acc_first * scale_first[..., None] + acc_second * scale_second[..., None]
    return (row_top, row_sum, numerator)


def append_rows(cache_block, tree_all, choose, slot_map, written):
    picked = jnp.einsum(
        "rjn,rnhe->rjhe", choose, tree_all, preferred_element_type=jnp.float32
    ).astype(jnp.bfloat16)
    placed = jnp.einsum(
        "rjp,rjhe->rphe", slot_map, picked, preferred_element_type=jnp.float32
    ).astype(jnp.bfloat16)
    return jnp.where(written[:, :, None, None], placed, cache_block)


def on_device_plain(
    tree_queries,
    tree_keys,
    tree_values,
    cache_keys,
    cache_values,
    out_weight,
    context_lengths,
    parents,
    accepted_nodes,
    accepted_count,
):
    requests, ctx_local, kv_local, head_dim = cache_keys.shape
    node_local, q_local = (tree_queries.shape[1], tree_queries.shape[2])
    group_size = q_local // kv_local
    path_len = accepted_nodes.shape[1]
    scale_factor = 1.0 / math.sqrt(head_dim)
    seq_index = lax.axis_index("seq")
    seq_count = lax.axis_size("seq")
    nodes_all = node_local * seq_count
    offset = seq_index * ctx_local
    grouped = tree_queries.reshape(requests, node_local, kv_local, group_size, head_dim)
    tree_all_k, tree_all_v = (
        lax.all_gather(tree_keys, "seq", axis=1, tiled=True),
        lax.all_gather(tree_values, "seq", axis=1, tiled=True),
    )
    closure = ancestors(parents)
    home_rows = lax.dynamic_slice_in_dim(closure, seq_index * node_local, node_local, 1)
    tree_state = partial_attention(
        grouped, tree_all_k, tree_all_v, home_rows[:, :, None, None, :] > 0.5, scale_factor
    )
    positions = offset + jnp.arange(ctx_local, dtype=jnp.int32)
    usable = (positions[None, :] < context_lengths[:, None])[:, None, None, None, :]
    everyone = lax.all_gather(grouped, "seq", axis=1, tiled=True)
    row_top, row_sum, numerator = partial_attention(
        everyone, cache_keys, cache_values, usable, scale_factor
    )
    highest = lax.pmax(row_top, "seq")
    factor = jnp.exp(row_top - highest)
    summed_acc, summed_sum = (
        lax.psum_scatter(numerator * factor[..., None], "seq", scatter_dimension=1, tiled=True),
        lax.psum_scatter(row_sum * factor, "seq", scatter_dimension=1, tiled=True),
    )
    home_top = lax.dynamic_slice_in_dim(highest, seq_index * node_local, node_local, 1)
    cache_state = (home_top, summed_sum, summed_acc)
    final_top, final_sum, final_acc = merge_parts(cache_state, tree_state)
    attention = (
        (final_acc / final_sum[..., None])
        .astype(jnp.bfloat16)
        .reshape(requests, node_local, q_local * head_dim)
    )
    partial_terms = jnp.einsum(
        "rnx,xd->rnd",
        lax.all_gather(attention, "seq", axis=1, tiled=True),
        out_weight,
        preferred_element_type=jnp.float32,
    )
    partial_terms = partial_terms.reshape(requests * nodes_all, out_weight.shape[1])
    projected = lax.psum_scatter(partial_terms, "head", scatter_dimension=0, tiled=True).astype(
        jnp.bfloat16
    )
    choose = (
        accepted_nodes[:, :, None] == jnp.arange(nodes_all, dtype=jnp.int32)[None, None, :]
    ).astype(jnp.bfloat16)
    steps_index = jnp.arange(path_len, dtype=jnp.int32)
    targets = context_lengths[:, None] + steps_index[None, :] - offset
    alive = steps_index[None, :] < accepted_count[:, None]
    slot_flags = (
        targets[:, :, None] == jnp.arange(ctx_local, dtype=jnp.int32)[None, None, :]
    ) & alive[:, :, None]
    slot_map = slot_flags.astype(jnp.bfloat16)
    written = jnp.sum(slot_flags.astype(jnp.float32), axis=1) > 0.5
    keys_out = append_rows(cache_keys, tree_all_k, choose, slot_map, written)
    values_out = append_rows(cache_values, tree_all_v, choose, slot_map, written)
    return (projected, keys_out, values_out)


MESH = pl.DeviceIdType.MESH
LOG2E = math.log2(math.e)


def bit_of(me, bit):
    return (me // (1 << bit)) % 2


def partner_of(me, bit):
    return me + (1 - 2 * bit_of(me, bit)) * (1 << bit)


def greet(me, levels):
    barrier = pltpu.get_barrier_semaphore()
    for bit in range(levels):
        pl.semaphore_signal(
            barrier, inc=1, device_id={"seq": partner_of(me, bit)}, device_id_type=MESH
        )
    pl.semaphore_wait(barrier, levels)


def gather_orders(levels):
    high = list(range(levels - 1, 2, -1))
    return (high + [1, 2, 0], high + [2, 1, 0])


def digits_of(value, levels):
    return tuple((value // (1 << bit)) % 2 for bit in range(levels - 1, -1, -1))


def gather_place(own, orders, c, p, half):
    levels = len(own)
    done = orders[half][:p]
    return (
        (c,)
        + tuple(slice(None) if bit in done else own[bit] for bit in range(levels - 1, -1, -1))
        + (half,)
    )


def gather_copy(me, own, orders, mine, out, sems, c, p, half):
    place = gather_place(own, orders, c, p, half)
    return pltpu.make_async_remote_copy(
        src_ref=mine.at[c, half] if p == 0 else out.at[place],
        dst_ref=out.at[place],
        send_sem=sems[0].at[c, p, half],
        recv_sem=sems[1].at[c, p, half],
        device_id={"seq": partner_of(me, orders[half][p])},
        device_id_type=MESH,
    )


def wavefront(chunks, levels):
    return [
        (step, step - p, p)
        for step in range(chunks + levels)
        for p in range(levels, 0, -1)
        if 0 <= step - p < chunks
    ]


def project_kernel(levels, kv, cuts, mine, weight, out, held, weights, total, own_sem, send_sem, recv_sem, weight_sem):
    me = lax.axis_index("seq")
    orders = gather_orders(levels)
    own = [bit_of(me, bit) for bit in range(levels)]
    chunks, _, half_rows, width = mine.shape
    depth = weight.shape[0] // kv
    loads = [
        pltpu.make_async_copy(
            weight.at[pl.ds(h * depth, depth)], weights.at[pl.ds(h * depth, depth)], weight_sem.at[h]
        )
        for h in range(kv)
    ]
    greet(me, levels)
    copy = functools.partial(gather_copy, me, own, orders, mine, held, (send_sem, recv_sem))
    own_place = digits_of(me, levels)
    locals_ = [
        pltpu.make_async_copy(mine.at[c], held.at[(c,) + own_place], own_sem.at[c])
        for c in range(chunks)
    ]

    for c in range(chunks):
        for half in range(2):
            copy(c, 0, half).start()
    for one in locals_ + loads:
        one.start()

    kv_levels = kv.bit_length() - 1
    parts = 1 << (levels - kv_levels)
    group = depth // width
    requests = chunks // cuts
    some = cuts * 2 * half_rows // group

    def multiply(first, last):
        rows = (last - first) * parts * some
        at = first * parts * some

        def body(h, carry):
            term = None
            for g in range(0, group, 2):
                sides = []
                for i in (g, g + 1):
                    cut, start = divmod(i * some, 2 * half_rows)
                    half, start = divmod(start, half_rows)
                    pieces = [
                        held[(r * cuts + cut,) + digits_of(h, kv_levels) + digits_of(part, levels - kv_levels) + (half, pl.ds(start, some))]
                        for r in range(first, last)
                        for part in range(parts)
                    ]
                    sides.append(jnp.concatenate(pieces, axis=0))
                left = jnp.concatenate(sides, axis=1)
                right = weights[pl.ds(pl.multiple_of(h * depth + g * width, width), 2 * width), :]
                now = jnp.dot(left, right, preferred_element_type=jnp.float32)
                term = now if term is None else term + now
            total[at : at + rows, :] += term
            return carry

        total[at : at + rows, :] = jnp.zeros((rows, total.shape[1]), jnp.float32)
        lax.fori_loop(0, kv, body, 0)
        out[at : at + rows, :] = total[at : at + rows, :].astype(out.dtype)

    for _, c, p in wavefront(chunks, levels):
        if p == 1:
            locals_[c].wait()
        for half in range(2):
            copy(c, p - 1, half).wait_recv()
            if p < levels:
                copy(c, p, half).start()
        if p == levels - 1 and c == chunks - 1:
            for one in loads:
                one.wait()
            multiply(0, requests - 1)
    multiply(requests - 1, requests)
    for c in range(chunks):
        for p in range(levels):
            for half in range(2):
                copy(c, p, half).wait_send()


def gather_project(block, weight, count, kv, cuts, collective_id):
    chunks, _, half_rows, width = block.shape
    levels = count.bit_length() - 1
    columns = weight.shape[1]
    rows = chunks * count * 2 * half_rows * width // weight.shape[0]
    return pl.pallas_call(
        functools.partial(project_kernel, levels, kv, cuts),
        out_shape=jax.ShapeDtypeStruct((rows, columns), jnp.bfloat16),
        in_specs=[pl.BlockSpec(memory_space=pl.ANY)] * 2,
        out_specs=pl.BlockSpec(memory_space=pltpu.VMEM),
        scratch_shapes=[
            pltpu.VMEM((chunks,) + (2,) * levels + block.shape[1:], block.dtype),
            pltpu.VMEM(weight.shape, weight.dtype),
            pltpu.VMEM((rows, columns), jnp.float32),
            pltpu.SemaphoreType.DMA((chunks,)),
            pltpu.SemaphoreType.DMA((chunks, levels, 2)),
            pltpu.SemaphoreType.DMA((chunks, levels, 2)),
            pltpu.SemaphoreType.DMA((kv,)),
        ],
        compiler_params=pltpu.CompilerParams(
            collective_id=collective_id, has_side_effects=True, vmem_limit_bytes=40 * 2**20
        ),
    )(block, weight)


def attend_kernel(
    scale, levels,
    lengths, mine, k, v, own_bias, out, tree,
    everyone, k_held, v_held, k_wide, v_wide, tree_wide,
    work, work_s, keep, own_sem, send_sem, recv_sem, cache_sem, tree_sem, out_send, out_recv,
    *held_all,
):
    me = lax.axis_index("seq")
    orders = gather_orders(levels)
    backward = tuple(order[::-1] for order in orders)
    own = [bit_of(me, bit) for bit in range(levels)]
    held, held_s = held_all[:levels], held_all[levels:]
    requests, ctx, kv, width = k.shape
    group = (mine.shape[2] - 2 * kv) // kv
    heads = group * kv
    count = 1 << levels
    nodes = 2 * count
    parts = count // kv
    tile = 2 * width
    offset = me * ctx

    copy = functools.partial(gather_copy, me, own, orders, mine, everyone, (send_sem, recv_sem))
    own_place = digits_of(me, levels)
    loads = [
        [
            pltpu.make_async_copy(source.at[r], target.at[r], cache_sem.at[kind, r])
            for kind, (source, target) in enumerate(((k, k_held), (v, v_held)))
        ]
        for r in range(requests)
    ]

    def own_copy(c):
        return pltpu.make_async_copy(mine.at[c], everyone.at[(c,) + own_place], own_sem.at[c])

    def tree_copy(c):
        spread = (slice(None),) * (levels + 1)
        return pltpu.make_async_copy(
            everyone.at[(c,) + spread + (pl.ds(heads, 2 * kv),)], tree.at[c], tree_sem.at[c]
        )

    greet(me, levels)

    def begin(c):
        if c < requests:
            for half in range(2):
                copy(c, 0, half).start()

    begin(0)
    begin(1)
    for c in range(requests):
        own_copy(c).start()
    for r in range(requests):
        for one in loads[r]:
            one.start()

    def forward(c, p):
        if p == 1:
            own_copy(c).wait()
        for half in range(2):
            copy(c, p - 1, half).wait_recv()
            if p < levels:
                copy(c, p, half).start()
        if p == levels:
            tree_copy(c).start()

    diagonal = lax.broadcasted_iota(jnp.int32, (width, width), 0) == lax.broadcasted_iota(
        jnp.int32, (width, width), 1
    )

    def score(rows, key):
        return lax.dot_general(
            rows, key, (((1,), (1,)), ((), ())), preferred_element_type=jnp.float32
        )

    def block(scores, value, bias):
        scores = scores * (scale * LOG2E) + bias
        top = jnp.max(scores, axis=1, keepdims=True)
        weights = jnp.exp2(scores - top)
        total = jnp.sum(weights, axis=1, keepdims=True)
        number = jnp.dot(weights.astype(jnp.bfloat16), value, preferred_element_type=jnp.float32)
        return top, total, number

    def widen(r):
        for kind, (cache, rows, wide) in enumerate(((k, k_held, k_wide), (v, v_held, v_wide))):
            pltpu.make_async_copy(cache.at[r], rows.at[r], cache_sem.at[kind, r]).wait()
            wide[...] = rows[r].astype(jnp.float32).reshape(ctx * kv, width)

    def attention(r, h):
        pl.when((h == 0) & (r > 0))(functools.partial(widen, r))
        keys = k_wide[pl.ds(h, ctx, stride=kv), :].astype(jnp.bfloat16)
        values = v_wide[pl.ds(h, ctx, stride=kv), :].astype(jnp.bfloat16)
        position = offset + lax.broadcasted_iota(jnp.int32, (1, ctx), 1)
        bias = jnp.where(position < lengths[r], 0.0, NEG)
        everything = (slice(None),) * (levels + 1)

        def queries(part):
            low = levels - (parts.bit_length() - 1)
            where = digits_of(part, levels - low) + (slice(None),) * (low + 1)
            found = everyone[(r,) + where + (pl.ds(pl.multiple_of(h * group, group), group),)]
            return found.reshape(tile, width)

        def store(part, top, total, number):
            number = (number * (1.0 / total)).astype(jnp.bfloat16)
            lines = top + jnp.log2(total)
            place = (r,) + digits_of(h * parts + part, levels)
            for half in range(2):
                span = slice(half * width, (half + 1) * width)
                work[place + (half,)] = number[span]
                work_s[place + (half,)] = jnp.sum(
                    jnp.where(diagonal, lines[span], 0.0), axis=0, keepdims=True
                )

        ahead = score(queries(0), keys)
        for part in range(parts):
            scores = ahead
            if part + 1 < parts:
                ahead = score(queries(part + 1), keys)
            store(part, *block(scores, values, bias))

        @pl.when(r * kv + h == me)
        def _():
            tree_wide[...] = (
                everyone[(r,) + everything + (pl.ds(heads, 2 * kv),)]
                .astype(jnp.float32)
                .reshape(nodes * 2 * kv, width)
            )
            own_k = tree_wide[pl.ds(h, nodes, stride=2 * kv), :].astype(jnp.bfloat16)
            own_v = tree_wide[pl.ds(kv + h, nodes, stride=2 * kv), :].astype(jnp.bfloat16)
            for part in range(parts):
                rows = queries(part)
                top, total, number = block(score(rows, keys), values, bias)
                t_top, t_total, t_number = block(
                    score(rows, own_k), own_v, own_bias[part * tile : (part + 1) * tile]
                )
                high = jnp.maximum(top, t_top)
                fa, fb = jnp.exp2(top - high), jnp.exp2(t_top - high)
                store(part, high, total * fa + t_total * fb, number * fa + t_number * fb)

    def send(c, p, half):
        bit_now = backward[half][p]
        done = backward[half][:p]
        where = tuple(
            own[bit] if bit in done else 1 - own[bit] if bit == bit_now else slice(None)
            for bit in range(levels - 1, -1, -1)
        )
        place = (c,) + where + (half,)
        return [
            pltpu.make_async_remote_copy(
                src_ref=source.at[place],
                dst_ref=target.at[c, half],
                send_sem=out_send.at[kind, c, p, half],
                recv_sem=out_recv.at[kind, c, p, half],
                device_id={"seq": partner_of(me, bit_now)},
                device_id_type=MESH,
            )
            for kind, (source, target) in enumerate(((work, held[p]), (work_s, held_s[p])))
        ]

    def merge(c, p, half):
        order = backward[half]
        done = order[: p + 1]
        last = p == levels - 1

        def one(k, kept):
            fixed = {bit: own[bit] for bit in done}
            if not last:
                fixed[order[p + 1]] = own[order[p + 1]] if kept else 1 - own[order[p + 1]]
            free = [bit for bit in range(levels - 1, -1, -1) if bit not in fixed]
            for rank, bit in enumerate(reversed(free)):
                fixed[bit] = (k // (1 << rank)) % 2
            at_work = (c,) + tuple(fixed[bit] for bit in range(levels - 1, -1, -1)) + (half,)
            at_held = (c, half) + tuple(
                fixed[bit] for bit in range(levels - 1, -1, -1) if bit not in done
            )
            at_keep = (c, half) + tuple(
                fixed[bit] for bit in range(levels - 1, -1, -1) if bit not in order[:2]
            )
            log_a, log_b = work_s[at_work], held_s[p][at_held]
            top = jnp.maximum(log_a, log_b)
            part_a, part_b = jnp.exp2(log_a - top), jnp.exp2(log_b - top)
            total = part_a + part_b
            share = jnp.sum(jnp.where(diagonal, part_a / total, 0.0), axis=1, keepdims=True)
            here = work[at_work].astype(jnp.float32) if p == 0 else keep[at_keep]
            merged = here * share + held[p][at_held].astype(jnp.float32) * (1.0 - share)
            if last:
                out[c, half] = merged.astype(jnp.bfloat16)
                return
            if kept:
                keep[at_keep] = merged
            else:
                work[at_work] = merged.astype(jnp.bfloat16)
            work_s[at_work] = top + jnp.log2(total)

        if last:
            one(0, True)
            return
        for kept in (False, True):
            size = 1 << (levels - 2 - p)
            if size == 1:
                one(0, kept)
            else:
                lax.fori_loop(0, size, lambda k, carry, kept=kept: (one(k, kept), carry)[1], 0)
            if not kept:
                for pending in send(c, p + 1, half):
                    pending.start()

    def reduce(c, p):
        for half in range(2):
            if p == 0:
                for one in send(c, 0, half):
                    one.start()
            else:
                for one in send(c, p - 1, half):
                    one.wait_recv()
                merge(c, p - 1, half)

    events = []
    late = {}
    for step, c, p in wavefront(requests, levels):
        if step <= levels:
            if (c, p) == (0, levels):
                widen(0)
            forward(c, p)
            if p == 1:
                begin(step + 1)
        else:
            late.setdefault(step, []).append((c, p))
    for step, found in late.items():
        after = step - levels
        for c, p in found:
            if p == levels:
                slot = c * kv - 1
            else:
                slot = min((after - 1) * kv + (3 if p == levels - 1 else 1), c * kv - 2)
            events.append((slot, 0, -c, functools.partial(forward, c, p)))
    for c in range(requests):
        base = (c + 1) * kv - 1
        for p, wait in enumerate((0, 2, 7, 11, 13, 15)[: levels + 1]):
            events.append((base + wait, 1, -c, functools.partial(reduce, c, p)))
    events.sort(key=lambda e: e[:3])
    total_steps = requests * kv

    def step_body(i, carry):
        attention(i // kv, i % kv)
        for slot, _, _, act in events:
            if slot < total_steps:
                pl.when(i == slot)(act)
        return carry

    lax.fori_loop(0, total_steps, step_body, 0)
    for slot, _, _, act in events:
        if slot >= total_steps:
            act()
    for c in range(requests):
        tree_copy(c).wait()
        for p in range(levels):
            for half in range(2):
                copy(c, p, half).wait_send()
                for one in send(c, p, half):
                    one.wait_send()


def attend(scale, count, lengths, mine, k, v, own_bias, collective_id):
    requests, ctx, kv, width = k.shape
    levels = count.bit_length() - 1
    bits = (2,) * levels
    rows = 2 * mine.shape[2] - 4 * kv
    half_rows = rows // 2
    work = requests * kv * own_bias.shape[0] * ctx
    hbm = pl.BlockSpec(memory_space=pl.ANY)
    vmem = pl.BlockSpec(memory_space=pltpu.VMEM)
    held = [
        pltpu.VMEM((requests, 2) + bits[: levels - 1 - p] + (half_rows, width), jnp.bfloat16)
        for p in range(levels)
    ]
    held_s = [
        pltpu.VMEM((requests, 2) + bits[: levels - 1 - p] + (1, half_rows), jnp.float32)
        for p in range(levels)
    ]
    return pl.pallas_call(
        functools.partial(attend_kernel, scale, levels),
        in_specs=[pl.BlockSpec(memory_space=pltpu.SMEM), hbm, hbm, hbm, vmem],
        out_specs=[vmem, hbm],
        out_shape=[
            jax.ShapeDtypeStruct((requests, 2, half_rows, width), jnp.bfloat16),
            jax.ShapeDtypeStruct((requests,) + bits + (2, 2 * kv, width), mine.dtype),
        ],
        scratch_shapes=[
            pltpu.VMEM((requests,) + bits + mine.shape[1:], mine.dtype),
            pltpu.VMEM(k.shape, k.dtype),
            pltpu.VMEM(v.shape, v.dtype),
            pltpu.VMEM((ctx * kv, width), jnp.float32),
            pltpu.VMEM((ctx * kv, width), jnp.float32),
            pltpu.VMEM((2 * count * 2 * kv, width), jnp.float32),
            pltpu.VMEM((requests,) + bits + (2, half_rows, width), jnp.bfloat16),
            pltpu.VMEM((requests,) + bits + (2, 1, half_rows), jnp.float32),
            pltpu.VMEM((requests, 2) + bits[2:] + (half_rows, width), jnp.float32),
            pltpu.SemaphoreType.DMA((requests,)),
            pltpu.SemaphoreType.DMA((requests, levels, 2)),
            pltpu.SemaphoreType.DMA((requests, levels, 2)),
            pltpu.SemaphoreType.DMA((2, requests)),
            pltpu.SemaphoreType.DMA((requests,)),
            pltpu.SemaphoreType.DMA((2, requests, levels, 2)),
            pltpu.SemaphoreType.DMA((2, requests, levels, 2)),
        ]
        + held
        + held_s,
        compiler_params=pltpu.CompilerParams(
            collective_id=collective_id, has_side_effects=True, vmem_limit_bytes=60 * 2**20
        ),
        cost_estimate=pl.CostEstimate(
            flops=4 * work * width, bytes_accessed=4 * k.size * 2, transcendentals=work
        ),
    )(lengths, mine, k, v, own_bias)


def append_kernel(where, lengths, accepted, count, k, v, tree, k_out, v_out):
    r = pl.program_id(0)
    ctx, kv = k.shape[1:3]
    start = where[0] + pl.program_id(1) * ctx
    for kind, (cache, target) in enumerate(((k, k_out), (v, v_out))):
        target[...] = cache[...]
        for j in range(accepted.shape[1]):
            slot = lengths[r] + j - start

            @pl.when((j < count[r]) & (slot >= 0) & (slot < ctx))
            def _():
                target[0, slot] = tree[0, accepted[r, j], kind]


def append(where, lengths, accepted, count, k, v, tree):
    requests, ctx, kv, width = k.shape
    cuts = 2 if ctx % 2 == 0 else 1
    cache = pl.BlockSpec((1, ctx // cuts, kv, width), lambda r, b, *_: (r, b, 0, 0))
    return pl.pallas_call(
        append_kernel,
        grid_spec=pltpu.PrefetchScalarGridSpec(
            num_scalar_prefetch=4,
            grid=(requests, cuts),
            in_specs=[
                cache, cache,
                pl.BlockSpec((1,) + tree.shape[1:], lambda r, b, *_: (r, 0, 0, 0, 0)),
            ],
            out_specs=[cache, cache],
        ),
        out_shape=[jax.ShapeDtypeStruct(k.shape, k.dtype)] * 2,
        compiler_params=pltpu.CompilerParams(vmem_limit_bytes=60 * 2**20),
    )(where, lengths, accepted, count, k, v, tree)


def on_device(
    tree_queries,
    tree_keys,
    tree_values,
    cache_keys,
    cache_values,
    out_weight,
    context_lengths,
    parents,
    accepted_nodes,
    accepted_count,
):
    requests, ctx, kv, width = cache_keys.shape
    node_local, heads = tree_queries.shape[1:3]
    group = heads // kv
    count = lax.axis_size("seq")
    nodes = node_local * count
    part = kv * nodes // count
    me = lax.axis_index("seq")
    sent = jnp.concatenate([tree_queries, tree_keys, tree_values], axis=2)
    own_request = lax.rem(me, requests * kv) // kv
    own_reach = lax.dynamic_index_in_dim(ancestors(parents), own_request, 0, keepdims=False)
    own_bias = jnp.repeat(jnp.where(own_reach > 0.5, 0.0, NEG), group, axis=0)
    home, tree = attend(
        1.0 / math.sqrt(width), count, context_lengths, sent, cache_keys, cache_values, own_bias, 1
    )
    home = home.reshape(requests, part, group, width).swapaxes(1, 2)
    cuts = 1
    projected = gather_project(
        home.reshape(requests * cuts, 2, part * group // (2 * cuts), width),
        out_weight, count, kv, cuts, 2,
    )
    keys_out, values_out = append(
        (me * ctx).astype(jnp.int32).reshape(1),
        context_lengths, accepted_nodes, accepted_count, cache_keys, cache_values,
        tree.reshape(requests, nodes, 2, kv, width),
    )
    return (projected, keys_out, values_out)


def fits(mesh, args):
    queries, keys = args[0], args[3]
    count, split = mesh.shape["seq"], mesh.shape["head"]
    requests, nodes, heads, width = queries.shape
    kv = keys.shape[2]
    rows = nodes * heads // count
    return (
        split == 1
        and count >= 8
        and count & (count - 1) == 0
        and count % kv == 0
        and count >= requests * kv
        and nodes * kv // count % 16 == 0
        and nodes == 2 * count
        and rows == 2 * width
    )


def solution(mesh):
    in_specs = (
        P(None, "seq", "head", None),
        P(None, "seq", "head", None),
        P(None, "seq", "head", None),
        P(None, "seq", "head", None),
        P(None, "seq", "head", None),
        P("head", "seq"),
        P(),
        P(),
        P(),
        P(),
    )
    out_specs = (P("head", "seq"), P(None, "seq", "head", None), P(None, "seq", "head", None))

    def run(*args):
        body = on_device if fits(mesh, args) else on_device_plain
        return jax.shard_map(
            body, mesh=mesh, in_specs=in_specs, out_specs=out_specs, check_vma=False
        )(*args)

    return run
```
